128 devices in a mesh: gz: 32 (over z, x, y_hi), gy: 4 (over y_lo, core).
Axes of the slice: x: 4, y: 4 (y_hi: 2, y_lo: 2; y = y_hi * 2 + y_lo), z: 4, core: 2. Of those that a mesh axis runs over, the one named last changes fastest.
Arguments:
- features: bfloat16 [32, 64, 32, 256], P(None, 'gz', 'gy'), may hold values from -6 to 6
- w_enc: bfloat16 [27, 32, 32], replicated, may hold values from -0.21875 to 0.21875
- w_mid: bfloat16 [27, 64, 32], replicated, may hold values from -0.21875 to 0.21875
- w_dec: bfloat16 [27, 32, 96], replicated, may hold values from -0.125 to 0.125
- cotangent: bfloat16 [32, 64, 32, 256], P(None, 'gz', 'gy'), may hold values from -6 to 6
Outputs:
- decoded: bfloat16 [32, 64, 32, 256], P(None, 'gz', 'gy')
- grad_enc: float32 [27, 32, 32], replicated
- grad_mid: float32 [27, 64, 32], replicated
- grad_dec: float32 [27, 32, 96], replicated
The draws below stay inside these ranges and needn't reach their ends.
All inputs are finite; a program needn't handle non-finite values.
Results may differ from the reference program's by a relative error of at most 0.013.
Values may be sent and summed in bfloat16 or wider, within the bound.
A program may use at most 128 MiB of HBM per device.

```python
import jax
import jax.numpy as jnp
from jax import lax

C1 = 32
C2 = 64
NX = 256
NZ = 64
NY = 32


def block_levels(own_key, dims, split, smallest, top_value):
    gain = 1.0
    for dim, shards_of in split:
        steps = jax.random.uniform(jax.random.fold_in(jax.random.fold_in(own_key, 6), dim), (shards_of,), jnp.float32, smallest / len(split), top_value / len(split))
        gain = gain * jnp.repeat(jnp.exp(steps), dims[dim] // shards_of).reshape((-1,) + (1,) * (len(dims) - 1 - dim))
    return gain


def gaussian(rng, extent, deviation, limit, split=(), dtype=jnp.bfloat16):
    array = deviation * jax.random.normal(rng, extent, jnp.float32)
    if split:
        array = array * block_levels(rng, extent, split, -0.22, 0.18)
    return jnp.clip(array, -limit, limit).astype(dtype)


def setup_inputs(seed: int = 0) -> dict:
    streams_of = jax.random.split(jax.random.key(seed), 6)
    return {
        "features": gaussian(streams_of[0], (C1, NZ, NY, NX), 1.0, 6.0, ((1, 32), (2, 4))),
        "w_enc": gaussian(streams_of[1], (27, C1, C1), (27 * C1) ** -0.5, 0.21875),
        "w_mid": gaussian(streams_of[2], (27, C2, C1), (27 * C1) ** -0.5, 0.21875),
        "w_dec": gaussian(streams_of[3], (27, C1, C2 + C1), (27 * (C1 + C2)) ** -0.5, 0.125),
        "cotangent": gaussian(streams_of[4], (C1, NZ, NY, NX), 1.0, 6.0, ((1, 32), (2, 4))),
    }


def conv(field, weight):
    outs, ins = (weight.shape[1], weight.shape[2])
    kernel = weight.astype(jnp.float32).reshape(3, 3, 3, outs, ins).transpose(3, 4, 0, 1, 2)
    result = lax.conv_general_dilated(field.astype(jnp.float32)[None], kernel, (1, 1, 1), 'SAME', dimension_numbers=('NCDHW', 'OIDHW', 'NCDHW'), precision=lax.Precision.HIGHEST)
    return result[0]

def silu_slope(value):
    sigma = jax.nn.sigmoid(value)
    return sigma * (1.0 + value * (1.0 - sigma))

def weight_grad(field, grad, weight):
    start = jnp.zeros(weight.shape, jnp.float32)
    result = jax.vjp(lambda w: conv(field, w), start)[1](grad.astype(jnp.float32))
    return result[0]

def input_grad(grad, weight, shape):
    start = jnp.zeros(shape, jnp.float32)
    result = jax.vjp(lambda v: conv(v, weight), start)[1](grad.astype(jnp.float32))
    return result[0]

def sum_blocks(field):
    chans, depth, height, width = field.shape
    return field.reshape(chans, depth // 2, 2, height // 2, 2, width // 2, 2).sum(axis=(2, 4, 6))

def upsample(field):
    chans, depth, height, width = field.shape
    wide = jnp.broadcast_to(field[:, :, None, :, None, :, None], (chans, depth, 2, height, 2, width, 2))
    return wide.reshape(chans, 2 * depth, 2 * height, 2 * width)

def reference(features, w_enc, w_mid, w_dec, cotangent):
    enc_pre = conv(features, w_enc)
    skip = jax.nn.silu(enc_pre).astype(jnp.bfloat16)
    pooled = (sum_blocks(skip.astype(jnp.float32)) * 0.125).astype(jnp.bfloat16)
    mid_pre = conv(pooled, w_mid)
    coarse = jax.nn.silu(mid_pre).astype(jnp.bfloat16)
    joined = jnp.concatenate([upsample(coarse), skip], axis=0)
    decoded = conv(joined, w_dec).astype(jnp.bfloat16)
    scale = (NZ * NY * NX) ** (-0.5)
    grad_dec = weight_grad(joined, cotangent, w_dec) * scale
    back_joined = input_grad(cotangent, w_dec, joined.shape)
    back_mid = (silu_slope(mid_pre) * sum_blocks(back_joined[:C2])).astype(jnp.bfloat16)
    grad_mid = weight_grad(pooled, back_mid, w_mid) * scale
    back_pool = input_grad(back_mid, w_mid, pooled.shape)
    back_enc = (silu_slope(enc_pre) * (back_joined[C2:] + upsample(back_pool) * 0.125)).astype(jnp.bfloat16)
    grad_enc = weight_grad(features, back_enc, w_enc) * scale
    return (decoded, grad_enc, grad_mid, grad_dec)
```

```python
import functools

import jax
import jax.numpy as jnp
from jax import lax
from jax.experimental import pallas as pl
from jax.experimental.pallas import tpu as pltpu
from jax.sharding import PartitionSpec as P

MESH = pl.DeviceIdType.MESH
BF = jnp.bfloat16
F32 = jnp.float32
DIRECTIONS = [(a, b) for a in (-1, 0, 1) for b in (-1, 0, 1) if (a, b) != (0, 0)]


def iota(shape, dim):
    return lax.broadcasted_iota(jnp.int32, shape, dim)


def hot(mask):
    return jnp.where(mask, 1.0, 0.0).astype(BF)


def dot(a, b):
    return jnp.dot(a, b, preferred_element_type=F32)


def dot_nt(a, b):
    return lax.dot_general(a, b, (((1,), (1,)), ((), ())), preferred_element_type=F32)


def rows_to_cells(chans, height):
    n = chans * height
    r, s = iota((n, n), 0), iota((n, n), 1)
    return hot(s == (r % chans) * height + r // chans)


def cells_to_rows(chans, height):
    n = chans * height
    r, s = iota((n, n), 0), iota((n, n), 1)
    return hot(r == (s % chans) * height + s // chans)


def split_four(width):
    half = width // 2
    r, s = iota((width, 2 * width), 0), iota((width, 2 * width), 1)
    return hot(r == 2 * (s % half) - 1 + s // half)


def shift_parity(width):
    half = width // 2
    r, s = iota((width, width), 0), iota((width, width), 1)
    c = s % half
    first = (s < half) & (c > 0) & (r == half + c - 1)
    second = (s >= half) & (c < half - 1) & (r == c + 1)
    return hot(first | second)


def shift_both(half):
    r, s = iota((half, 2 * half), 0), iota((half, 2 * half), 1)
    return hot(((s < half) & (r == s - 1)) | ((s >= half) & (r == s - half + 1)))


def merge_parity(width):
    half = width // 2
    r, s = iota((width, width), 0), iota((width, width), 1)
    return hot(s == 2 * (r % half) + r // half)


class Halo:
    def __init__(self, ref, send, recv, number, grid):
        self.ref, self.send, self.recv, self.number = ref, send, recv, number
        self.gz, self.gy, self.nz, self.ny = grid
        self.depth, self.height = ref.shape[0] - 2, ref.shape[1] - 2

    def exists(self, a, b):
        checks = []
        if a:
            checks.append(self.gz > 0 if a < 0 else self.gz < self.nz - 1)
        if b:
            checks.append(self.gy > 0 if b < 0 else self.gy < self.ny - 1)
        return functools.reduce(jnp.logical_and, checks)

    def source(self, d, n):
        return {-1: pl.ds(1, 1), 0: pl.ds(1, n), 1: pl.ds(n, 1)}[d]

    def target(self, d, n):
        return {-1: pl.ds(n + 1, 1), 0: pl.ds(1, n), 1: pl.ds(0, 1)}[d]

    def copy(self, i):
        a, b = DIRECTIONS[i]
        peer = (lax.rem(self.gz + a + self.nz, self.nz), lax.rem(self.gy + b + self.ny, self.ny))
        return pltpu.make_async_remote_copy(
            src_ref=self.ref.at[self.source(a, self.depth), self.source(b, self.height)],
            dst_ref=self.ref.at[self.target(a, self.depth), self.target(b, self.height)],
            send_sem=self.send.at[self.number, i],
            recv_sem=self.recv.at[self.number, i],
            device_id=peer,
            device_id_type=MESH,
        )

    def start(self):
        for i in (1, 6, 3, 4, 0, 2, 5, 7):
            pl.when(self.exists(*DIRECTIONS[i]))(lambda i=i: self.copy(i).start())

    def clear(self):
        for i, (a, b) in enumerate(DIRECTIONS):
            @pl.when(jnp.logical_not(self.exists(-a, -b)))
            def _(a=a, b=b):
                part = self.ref.at[self.target(a, self.depth), self.target(b, self.height)]
                part[...] = jnp.zeros(part.shape, part.dtype)

    def arrived(self):
        for i, (a, b) in enumerate(DIRECTIONS):
            pl.when(self.exists(-a, -b))(lambda i=i: self.copy(i).wait_recv())

    def sent(self):
        for i, (a, b) in enumerate(DIRECTIONS):
            pl.when(self.exists(a, b))(lambda i=i: self.copy(i).wait_send())


class Group:
    def __init__(self, size, me, peer):
        self.size, self.me, self.peer = size, me, peer

    def others(self):
        return [lax.rem(self.me + d, self.size) for d in range(1, self.size)]


class Total:
    def __init__(self, first, second, mine, one, two, whole, sems):
        self.first, self.second = first, second
        self.mine, self.one, self.two, self.whole = mine, one, two, whole
        self.send1, self.recv1, self.send2, self.recv2, self.send3, self.recv3 = sems

    def copy(self, src, dst, send, recv, slot, peer):
        return pltpu.make_async_remote_copy(
            src_ref=src, dst_ref=dst, send_sem=send, recv_sem=recv,
            device_id=peer, device_id_type=MESH,
        )

    def step1(self, t, incoming):
        g = self.first
        slot = t if incoming else g.me
        return self.copy(self.mine.at[t], self.one.at[slot], self.send1.at[t], self.recv1.at[slot], slot, g.peer(t))

    def step2(self, t, incoming):
        g = self.second
        slot = t if incoming else g.me
        return self.copy(self.two.at[g.me], self.two.at[slot], self.send2.at[t], self.recv2.at[slot], slot, g.peer(t))

    def step3(self, t, incoming):
        g = self.first
        slot = t if incoming else g.me
        return self.copy(self.whole.at[g.me], self.whole.at[slot], self.send3.at[t], self.recv3.at[slot], slot, g.peer(t))

    def start1(self):
        for t in self.first.others():
            self.step1(t, False).start()

    def start2(self):
        total = self.mine[self.first.me].astype(F32)
        for t in self.first.others():
            self.step1(t, True).wait_recv()
            total = total + self.one[t].astype(F32)
        self.two[self.second.me] = total.astype(BF)
        for t in self.second.others():
            self.step2(t, False).start()

    def start3(self):
        for t in self.second.others():
            self.step2(t, True).wait_recv()
        total = self.two[0].astype(F32)
        for t in range(1, self.second.size):
            total = total + self.two[t].astype(F32)
        self.whole[self.first.me] = total.astype(BF)
        for t in self.first.others():
            self.step3(t, False).start()

    def finish(self):
        for t in self.first.others():
            self.step3(t, True).wait_recv()

    def drain(self):
        for t in self.first.others():
            self.step1(t, False).wait_send()
            self.step3(t, False).wait_send()
        for t in self.second.others():
            self.step2(t, False).wait_send()


def pair(ref, z, y, step=1):
    a = ref[pl.ds(z, 3), pl.ds(y, 3)]
    b = ref[pl.ds(z, 3), pl.ds(y + step, 3)]
    rows = 9 * ref.shape[2]
    return jnp.concatenate([a.reshape(rows, ref.shape[3]), b.reshape(rows, ref.shape[3])], axis=1)


def silu_slope(value):
    sigma = 1.0 / (1.0 + jnp.exp(-value))
    return sigma * (1.0 + value * (1.0 - sigma))


def silu(value):
    return value / (1.0 + jnp.exp(-value))


def kernel(
    nz, ny, scale,
    feat_ref, cot_ref, we_ref, wm_ref, ws_ref, wc_ref, wb_ref, wp_ref,
    decoded_ref, genc_ref, gmid_ref, gdec_ref,
    fh, ch, sh, ph, oh, bh,
    fx, cx, sx, px, ox, bx,
    slope, bskip, bsum, midp, joined, benc, dec_acc, enc_acc, mid_acc, dplane,
    a_mine, a_one, a_two, a_whole, b_mine, b_one, b_two, b_whole,
    hsend, hrecv, as1, ar1, as2, ar2, as3, ar3, bs1, br1, bs2, br2, bs3, br3,
):
    gz, gy = lax.axis_index("gz"), lax.axis_index("gy")
    c1, depth, height, width = feat_ref.shape
    half = width // 2
    c2 = bsum.shape[1]
    chigh = height // 2
    grid = (gz, gy, nz, ny)
    fhalo, chalo, shalo, phalo, ohalo, bhalo = [
        Halo(ref, hsend, hrecv, n, grid) for n, ref in enumerate((fh, ch, sh, ph, oh, bh))
    ]
    column = Group(2 * ny, lax.rem(gz, 2) * ny + gy, lambda t: (gz - lax.rem(gz, 2) + t // ny, lax.rem(t, ny)))
    plane = Group(nz // 2, gz // 2, lambda t: (2 * t + lax.rem(gz, 2), gy))

    barrier = pltpu.get_barrier_semaphore()
    away = gz + 2 * lax.rem(gz, 2) - 1
    arrivals = column.size + plane.size - 2
    for b in (-1, 0, 1):
        near = (away >= 0) & (away < nz) & (gy + b >= 0) & (gy + b < ny)
        arrivals = arrivals + jnp.where(near, 1, 0)

        @pl.when(near)
        def _(b=b):
            pl.semaphore_signal(barrier, inc=1, device_id=(away, gy + b), device_id_type=MESH)
    for group in (column, plane):
        for t in group.others():
            pl.semaphore_signal(barrier, inc=1, device_id=group.peer(t), device_id_type=MESH)

    to_cells = rows_to_cells(c1, height)
    for src, dst in ((feat_ref, fh), (cot_ref, ch)):
        for z in range(depth):
            own = src[:, z].astype(F32).reshape(c1 * height, width).astype(BF)
            own = dot(to_cells, own).astype(BF).reshape(height, c1, width)
            dst[1 + z, pl.ds(1, height)] = own

    pl.semaphore_wait(barrier, arrivals)

    fhalo.start()
    chalo.start()
    for halo in (fhalo, chalo, shalo, phalo, ohalo, bhalo):
        halo.clear()
    a_mine[...] = jnp.zeros(a_mine.shape, BF)
    b_mine[...] = jnp.zeros(b_mine.shape, BF)
    joined[...] = jnp.zeros(joined.shape, BF)
    px[...] = jnp.zeros(px.shape, BF)
    dec_acc[...] = jnp.zeros(dec_acc.shape, F32)
    enc_acc[...] = jnp.zeros(enc_acc.shape, F32)
    mid_acc[...] = jnp.zeros(mid_acc.shape, F32)

    def four(src, dst):
        spread = split_four(width)

        def body(z, carry):
            rows = src[z].reshape((height + 2) * c1, width)
            out = dot(rows, spread).astype(BF).reshape(height + 2, c1, 2 * width)
            for j in range(4):
                dst[z, :, j * c1 : (j + 1) * c1, :] = out[:, :, j * half : (j + 1) * half]
            return carry

        lax.fori_loop(0, depth + 2, body, 0)

    fhalo.arrived()
    four(fh, fx)

    def encode(yc, carry):
        pool = jnp.zeros((c1, half), F32)
        for z in range(depth):
            pre = dot(we_ref[...], pair(fx, z, 2 * yc))
            act = silu(pre).astype(BF)
            der = silu_slope(pre)
            for p in range(2):
                cell = act[:, p * half : (p + 1) * half]
                slope[z, 2 * yc + p] = der[:, p * half : (p + 1) * half]
                for q in range(2):
                    part = cell[q * c1 : (q + 1) * c1]
                    sh[1 + z, 1 + 2 * yc + p, :, q * half : (q + 1) * half] = part
                    joined[z, 2 * yc + p, q * 128 + c2 : q * 128 + c2 + c1, :] = part
                    pool = pool + part.astype(F32)
        ph[1, 1 + yc] = (pool * 0.125).astype(BF)
        return carry

    lax.fori_loop(0, chigh, encode, 0)
    phalo.start()
    shalo.start()

    chalo.arrived()
    four(ch, cx)

    def backward(yc, carry):
        low = jnp.zeros((c2, half), F32)
        for z in range(depth):
            out = dot(wb_ref[...], pair(cx, z, 2 * yc))
            for p in range(2):
                for q in range(2):
                    part = out[q * (c1 + c2) : (q + 1) * (c1 + c2), p * half : (p + 1) * half]
                    low = low + part[:c2]
                    bskip[z, 2 * yc + p, q * c1 : (q + 1) * c1, :] = part[c2:]
        bsum[yc] = low
        return carry

    lax.fori_loop(0, chigh, backward, 0)

    sides = shift_both(half)

    def three(src, dst):
        chans = src.shape[2]
        rows = src[...].reshape(src.shape[0] * src.shape[1] * chans, half)
        out = dot(rows, sides).astype(BF).reshape(src.shape[0], src.shape[1], chans, 2 * half)
        dst[:, :, 0:chans, :] = out[..., :half]
        dst[:, :, chans : 2 * chans, :] = src[...]
        dst[:, :, 2 * chans : 3 * chans, :] = out[..., half:]

    phalo.arrived()
    three(ph, px)
    for yc in range(0, chigh, 2):
        pre = dot(wm_ref[...], pair(px, 0, yc))
        for p in range(2):
            cell = pre[:, p * half : (p + 1) * half]
            act = silu(cell).astype(BF)
            oh[1, 1 + yc + p] = act
            for z in range(depth):
                for r in range(2):
                    for q in range(2):
                        joined[z, 2 * (yc + p) + r, q * 128 : q * 128 + c2, :] = act
            bh[1, 1 + yc + p] = (silu_slope(cell) * bsum[yc + p]).astype(BF)
    bhalo.start()
    ohalo.start()

    def decoder_grad(yc, carry):
        for z in range(depth):
            own = jnp.concatenate([joined[z, 2 * yc], joined[z, 2 * yc + 1]], axis=1)
            for w in range(3):
                for v in range(3):
                    field = jnp.concatenate(
                        [cx[z + w, 2 * yc + v], cx[z + w, 2 * yc + 1 + v]], axis=1
                    )
                    dec_acc[3 * w + v] += dot_nt(field, own)
        return carry

    lax.fori_loop(0, chigh, decoder_grad, 0)
    for kk in range(9):
        for kx in range(3):
            a_mine[kk, kx * c1 : (kx + 1) * c1, :] = (
                dec_acc[8 - kk, (2 - kx) * c1 : (3 - kx) * c1, 0:128]
                + dec_acc[8 - kk, (3 - kx) * c1 : (4 - kx) * c1, 128:256]
            ).astype(BF)

    for yc in range(0, chigh, 2):
        own = jnp.concatenate([bh[1, 1 + yc], bh[1, 2 + yc]], axis=1)
        mid_acc[...] += dot_nt(own, pair(px, 0, yc))
    for n in range(18):
        kk, h = n // 2, n % 2
        a_mine[9 + n // 3, (n % 3) * 32 : (n % 3 + 1) * 32, :] = mid_acc[
            h * 32 : (h + 1) * 32, kk * 128 : (kk + 1) * 128
        ].astype(BF)
    a_total = Total(plane, column, a_mine, a_one, a_two, a_whole, (as1, ar1, as2, ar2, as3, ar3))
    a_total.start1()

    bhalo.arrived()
    three(bh, bx)
    for yc in range(0, chigh, 2):
        pool = dot(wp_ref[...], pair(bx, 0, yc)) * 0.125
        for p in range(2):
            up = pool[:, p * half : (p + 1) * half]
            up = jnp.concatenate([up, up], axis=0)
            for z in range(depth):
                for r in range(2):
                    y = 2 * (yc + p) + r
                    benc[z, y] = (slope[z, y] * (bskip[z, y] + up)).astype(BF)

    def encoder_grad(yc, carry):
        for z in range(depth):
            own = jnp.concatenate([benc[z, 2 * yc], benc[z, 2 * yc + 1]], axis=1)
            enc_acc[...] += dot_nt(own, pair(fx, z, 2 * yc))
        return carry

    lax.fori_loop(0, chigh, encoder_grad, 0)
    for kk in range(9):
        even = enc_acc[0:c1, kk * 128 : (kk + 1) * 128]
        odd = enc_acc[c1 : 2 * c1, kk * 128 : (kk + 1) * 128]
        piece = (even + pltpu.roll(odd, 128 - c1, 1)).astype(BF)
        for h in range(2):
            n = 2 * kk + h
            b_mine[n // 3, (n % 3) * 16 : (n % 3 + 1) * 16, :] = piece[h * 16 : (h + 1) * 16]
    b_total = Total(column, plane, b_mine, b_one, b_two, b_whole, (bs1, br1, bs2, br2, bs3, br3))
    b_total.start1()
    a_total.start2()

    shalo.arrived()
    turn = shift_parity(width)

    def four_skip(z, carry):
        rows = sh[z].reshape((height + 2) * c1, width)
        out = dot(rows, turn).astype(BF).reshape(height + 2, c1, width)
        sx[z, :, 0:c1, :] = out[:, :, :half]
        sx[z, :, c1 : 2 * c1, :] = sh[z, :, :, 0:half]
        sx[z, :, 2 * c1 : 3 * c1, :] = sh[z, :, :, half:width]
        sx[z, :, 3 * c1 : 4 * c1, :] = out[:, :, half:]
        return carry

    lax.fori_loop(0, depth + 2, four_skip, 0)
    ohalo.arrived()
    three(oh, ox)
    b_total.start2()
    a_total.start3()

    def decode(yc, carry):
        for z in range(depth):
            out = dot(ws_ref[...], pair(sx, z, 2 * yc))
            for p in range(2):
                field = ox[pl.ds(z, 2), pl.ds(yc + p, 2)].reshape(4 * 3 * c2, half)
                row = (out[:, p * half : (p + 1) * half] + dot(wc_ref[2 * z + p], field)).astype(BF)
                for q in range(2):
                    dplane[z, 2 * yc + p, :, q * half : (q + 1) * half] = row[q * c1 : (q + 1) * c1]
        return carry

    lax.fori_loop(0, chigh, decode, 0)
    to_rows = cells_to_rows(c1, height)
    merge = merge_parity(width)
    for z in range(depth):
        rows = dplane[z].reshape(height * c1, width)
        rows = dot(rows, merge).astype(BF)
        decoded_ref[:, z] = dot(to_rows, rows).reshape(c1, height, width).astype(BF)

    b_total.start3()
    a_total.finish()
    for kk in range(9):
        for kx in range(3):
            gdec_ref[3 * kk + kx] = a_whole[kk, kx * c1 : (kx + 1) * c1, 0 : c1 + c2].astype(F32) * scale
    for n in range(18):
        kk, h = n // 2, n % 2
        piece = a_whole[9 + n // 3, (n % 3) * 32 : (n % 3 + 1) * 32, :].astype(F32) * scale
        for kx in range(3):
            gmid_ref[3 * kk + kx, h * 32 : (h + 1) * 32, :] = piece[:, kx * 32 : (kx + 1) * 32]
    b_total.finish()
    for n in range(18):
        kk, h = n // 2, n % 2
        piece = b_whole[n // 3, (n % 3) * 16 : (n % 3 + 1) * 16, :].astype(F32) * scale
        for kx in range(3):
            genc_ref[3 * kk + kx, h * 16 : (h + 1) * 16, :] = piece[:, kx * 32 : (kx + 1) * 32]

    for halo in (fhalo, chalo, shalo, phalo, ohalo, bhalo):
        halo.sent()
    a_total.drain()
    b_total.drain()


def fine_weights(w):
    outs, ins = w.shape[1:]
    w = w.reshape(9, 3, outs, ins).transpose(2, 0, 1, 3).reshape(outs, 9, 3 * ins)
    even = jnp.pad(w, ((0, 0), (0, 0), (0, ins)))
    odd = jnp.pad(w, ((0, 0), (0, 0), (ins, 0)))
    return jnp.concatenate([even, odd], axis=0).reshape(2 * outs, 9 * 4 * ins)


def coarse_weights(w, slots):
    outs, ins = w.shape[1:]
    w = w.reshape(9, 3, outs, ins).transpose(2, 0, 1, 3).reshape(outs, 9, 3 * ins)
    w = jnp.pad(w, ((0, 0), (0, 0), (0, (slots - 3) * ins)))
    return w.reshape(outs, 9 * slots * ins)


def flipped(w):
    return jnp.flip(w, 0).transpose(0, 2, 1)


def up_weights(w):
    outs, ins = w.shape[1:]
    w = w.astype(F32).reshape(3, 3, 3, outs, ins)

    def two(v, dim):
        a, b, c = (lax.index_in_dim(v, i, dim, keepdims=False) for i in range(3))
        return [[a, b + c], [a + b, c]]

    listed = []
    for z in two(w, 0):
        for y in zip(*[two(v, 0) for v in z]):
            rows = []
            for q in range(2):
                cols = []
                for cz in range(2):
                    for cy in range(2):
                        x = two(y[cz][cy], 0)[q]
                        blank = jnp.zeros_like(x[0])
                        cols += [x[0], x[1], blank] if q == 0 else [blank, x[0], x[1]]
                rows.append(jnp.concatenate(cols, axis=1))
            listed.append(jnp.concatenate(rows, axis=0))
    return jnp.stack(listed).astype(BF)


def local(features, w_enc, w_mid, w_dec, cotangent):
    nz, ny = lax.axis_size("gz"), lax.axis_size("gy")
    c1, depth, height, width = features.shape
    c2 = w_mid.shape[1]
    half, ch = width // 2, height // 2
    assert depth == 2 and c1 == 32 and c2 == 64 and half == 128
    we = fine_weights(w_enc)
    wm = coarse_weights(w_mid, 4)
    ws = fine_weights(w_dec[:, :, c2:])
    wc = up_weights(w_dec[:, :, :c2])
    wb = fine_weights(flipped(w_dec))
    wp = coarse_weights(flipped(w_mid), 3)
    scale = (depth * nz * height * ny * width) ** (-0.5)
    n1, n2 = nz // 2, 2 * ny
    vmem = pl.BlockSpec(memory_space=pltpu.VMEM)
    dma = pltpu.SemaphoreType.DMA
    fine, coarse = (depth + 2, height + 2), (3, ch + 2)
    decoded, genc, gmid, gdec = pl.pallas_call(
        functools.partial(kernel, nz, ny, scale),
        out_shape=(
            jax.ShapeDtypeStruct(features.shape, BF),
            jax.ShapeDtypeStruct(w_enc.shape, F32),
            jax.ShapeDtypeStruct(w_mid.shape, F32),
            jax.ShapeDtypeStruct(w_dec.shape, F32),
        ),
        in_specs=[vmem] * 8,
        out_specs=[vmem] * 4,
        scratch_shapes=[
            pltpu.VMEM(fine + (c1, width), BF),
            pltpu.VMEM(fine + (c1, width), BF),
            pltpu.VMEM(fine + (c1, width), BF),
            pltpu.VMEM(coarse + (c1, half), BF),
            pltpu.VMEM(coarse + (c2, half), BF),
            pltpu.VMEM(coarse + (c2, half), BF),
            pltpu.VMEM(fine + (4 * c1, half), BF),
            pltpu.VMEM(fine + (4 * c1, half), BF),
            pltpu.VMEM(fine + (4 * c1, half), BF),
            pltpu.VMEM(coarse + (4 * c1, half), BF),
            pltpu.VMEM(coarse + (3 * c2, half), BF),
            pltpu.VMEM(coarse + (3 * c2, half), BF),
            pltpu.VMEM((depth, height, 2 * c1, half), F32),
            pltpu.VMEM((depth, height, 2 * c1, half), F32),
            pltpu.VMEM((ch, c2, half), F32),
            pltpu.VMEM((ch, c2, half), F32),
            pltpu.VMEM((depth, height, 256, half), BF),
            pltpu.VMEM((depth, height, 2 * c1, half), BF),
            pltpu.VMEM((9, 4 * c1, 256), F32),
            pltpu.VMEM((2 * c1, 9 * 128), F32),
            pltpu.VMEM((c2, 9 * 128), F32),
            pltpu.VMEM((depth, height, c1, width), BF),
            pltpu.VMEM((n1, 96, 128), BF),
            pltpu.VMEM((n1, 96, 128), BF),
            pltpu.VMEM((n2, 96, 128), BF),
            pltpu.VMEM((n1, 96, 128), BF),
            pltpu.VMEM((n2, 48, 128), BF),
            pltpu.VMEM((n2, 48, 128), BF),
            pltpu.VMEM((n1, 48, 128), BF),
            pltpu.VMEM((n2, 48, 128), BF),
            dma((6, 8)), dma((6, 8)),
            dma((n1,)), dma((n1,)), dma((n2,)), dma((n2,)), dma((n1,)), dma((n1,)),
            dma((n2,)), dma((n2,)), dma((n1,)), dma((n1,)), dma((n2,)), dma((n2,)),
        ],
        compiler_params=pltpu.CompilerParams(
            collective_id=0, has_side_effects=True, vmem_limit_bytes=48 * 2**20
        ),
    )(features, cotangent, we, wm, ws, wc, wb, wp)
    return decoded, genc, gmid, gdec


def solution(mesh):
    placed = (P(None, "gz", "gy", None), P(), P(), P(), P(None, "gz", "gy", None))
    return jax.shard_map(
        local,
        mesh=mesh,
        in_specs=placed,
        out_specs=(P(None, "gz", "gy", None), P(), P(), P()),
        check_vma=False,
    )
```

```python
import functools

import jax
import jax.numpy as jnp
from jax import lax
from jax.experimental import pallas as pl
from jax.experimental.pallas import tpu as pltpu
from jax.sharding import PartitionSpec as P

MESH = pl.DeviceIdType.MESH
BF = jnp.bfloat16
F32 = jnp.float32
DIRECTIONS = [(a, b) for a in (-1, 0, 1) for b in (-1, 0, 1) if (a, b) != (0, 0)]


def iota(shape, dim):
    return lax.broadcasted_iota(jnp.int32, shape, dim)


def hot(mask):
    return jnp.where(mask, 1.0, 0.0).astype(BF)


def dot(a, b):
    return jnp.dot(a, b, preferred_element_type=F32)


def dot_nt(a, b):
    return lax.dot_general(a, b, (((1,), (1,)), ((), ())), preferred_element_type=F32)


def rows_to_cells(chans, height):
    n = chans * height
    r, s = iota((n, n), 0), iota((n, n), 1)
    return hot(s == (r % chans) * height + r // chans)


def cells_to_rows(chans, height):
    n = chans * height
    r, s = iota((n, n), 0), iota((n, n), 1)
    return hot(r == (s % chans) * height + s // chans)


def split_four(width):
    half = width // 2
    r, s = iota((width, 2 * width), 0), iota((width, 2 * width), 1)
    return hot(r == 2 * (s % half) - 1 + s // half)


def shift_parity(width):
    half = width // 2
    r, s = iota((width, width), 0), iota((width, width), 1)
    c = s % half
    first = (s < half) & (c > 0) & (r == half + c - 1)
    second = (s >= half) & (c < half - 1) & (r == c + 1)
    return hot(first | second)


def shift_both(half):
    r, s = iota((half, 2 * half), 0), iota((half, 2 * half), 1)
    return hot(((s < half) & (r == s - 1)) | ((s >= half) & (r == s - half + 1)))


def merge_parity(width):
    half = width // 2
    r, s = iota((width, width), 0), iota((width, width), 1)
    return hot(s == 2 * (r % half) + r // half)


def place(z, y):
    return (z - lax.rem(z, 2) + y // 2, 2 * lax.rem(y, 2) + lax.rem(z, 2))


def block(gz, gy):
    return gz - lax.rem(gz, 2) + lax.rem(gy, 2), 2 * lax.rem(gz, 2) + gy // 2


class Move:
    def __init__(self, src, dst, send, recv, peer, stays):
        self.src, self.dst, self.send, self.recv = src, dst, send, recv
        self.peer, self.stays = peer, stays

    def remote(self):
        return pltpu.make_async_remote_copy(
            src_ref=self.src, dst_ref=self.dst, send_sem=self.send, recv_sem=self.recv,
            device_id=self.peer, device_id_type=MESH,
        )

    def either(self, near, far):
        pl.when(self.stays)(lambda: near(pltpu.make_async_copy(self.src, self.dst, self.recv)))
        pl.when(jnp.logical_not(self.stays))(lambda: far(self.remote()))

    def start(self):
        self.either(lambda c: c.start(), lambda c: c.start())

    def wait_recv(self):
        self.either(lambda c: c.wait(), lambda c: c.wait_recv())

    def wait_send(self):
        pl.when(jnp.logical_not(self.stays))(lambda: self.remote().wait_send())


class Halo:
    def __init__(self, ref, send, recv, number, grid):
        self.ref, self.send, self.recv, self.number = ref, send, recv, number
        self.gz, self.gy, self.nz, self.ny = grid
        self.depth, self.height = ref.shape[0] - 2, ref.shape[1] - 2

    def exists(self, a, b):
        checks = []
        if a:
            checks.append(self.gz > 0 if a < 0 else self.gz < self.nz - 1)
        if b:
            checks.append(self.gy > 0 if b < 0 else self.gy < self.ny - 1)
        return functools.reduce(jnp.logical_and, checks)

    def source(self, d, n):
        return {-1: pl.ds(1, 1), 0: pl.ds(1, n), 1: pl.ds(n, 1)}[d]

    def target(self, d, n):
        return {-1: pl.ds(n + 1, 1), 0: pl.ds(1, n), 1: pl.ds(0, 1)}[d]

    def copy(self, i):
        a, b = DIRECTIONS[i]
        peer = place(lax.rem(self.gz + a + self.nz, self.nz), lax.rem(self.gy + b + self.ny, self.ny))
        return pltpu.make_async_remote_copy(
            src_ref=self.ref.at[self.source(a, self.depth), self.source(b, self.height)],
            dst_ref=self.ref.at[self.target(a, self.depth), self.target(b, self.height)],
            send_sem=self.send.at[self.number, i],
            recv_sem=self.recv.at[self.number, i],
            device_id=peer,
            device_id_type=MESH,
        )

    def start(self, listed=(1, 6, 3, 4, 0, 2, 5, 7)):
        for i in listed:
            pl.when(self.exists(*DIRECTIONS[i]))(lambda i=i: self.copy(i).start())

    def clear(self):
        for i, (a, b) in enumerate(DIRECTIONS):
            @pl.when(jnp.logical_not(self.exists(-a, -b)))
            def _(a=a, b=b):
                part = self.ref.at[self.target(a, self.depth), self.target(b, self.height)]
                part[...] = jnp.zeros(part.shape, part.dtype)

    def arrived(self):
        for i, (a, b) in enumerate(DIRECTIONS):
            pl.when(self.exists(-a, -b))(lambda i=i: self.copy(i).wait_recv())

    def sent(self):
        for i, (a, b) in enumerate(DIRECTIONS):
            pl.when(self.exists(a, b))(lambda i=i: self.copy(i).wait_send())


class Group:
    def __init__(self, size, me, peer, listed):
        self.size, self.me, self.peer, self.listed = size, me, peer, listed

    def others(self):
        return self.listed


class Total:
    def __init__(self, first, second, mine, one, two, whole, sems):
        self.first, self.second = first, second
        self.mine, self.one, self.two, self.whole = mine, one, two, whole
        self.send1, self.recv1, self.send2, self.recv2, self.send3, self.recv3 = sems

    def copy(self, src, dst, send, recv, slot, peer):
        return pltpu.make_async_remote_copy(
            src_ref=src, dst_ref=dst, send_sem=send, recv_sem=recv,
            device_id=peer, device_id_type=MESH,
        )

    def step1(self, t, incoming):
        g = self.first
        slot = t if incoming else g.me
        return self.copy(self.mine.at[t], self.one.at[slot], self.send1.at[t], self.recv1.at[slot], slot, g.peer(t))

    def step2(self, t, incoming):
        g = self.second
        slot = t if incoming else g.me
        return self.copy(self.two.at[g.me], self.two.at[slot], self.send2.at[t], self.recv2.at[slot], slot, g.peer(t))

    def step3(self, t, incoming):
        g = self.first
        slot = t if incoming else g.me
        return self.copy(self.whole.at[g.me], self.whole.at[slot], self.send3.at[t], self.recv3.at[slot], slot, g.peer(t))

    def start1(self):
        for t in self.first.others():
            self.step1(t, False).start()

    def start2(self):
        total = self.mine[self.first.me].astype(F32)
        for t in self.first.others():
            self.step1(t, True).wait_recv()
            total = total + self.one[t].astype(F32)
        self.two[self.second.me] = total.astype(BF)
        for t in self.second.others():
            self.step2(t, False).start()

    def start3(self):
        for t in self.second.others():
            self.step2(t, True).wait_recv()
        total = self.two[0].astype(F32)
        for t in range(1, self.second.size):
            total = total + self.two[t].astype(F32)
        self.whole[self.first.me] = total.astype(BF)
        for t in self.first.others():
            self.step3(t, False).start()

    def finish(self):
        for t in self.first.others():
            self.step3(t, True).wait_recv()

    def drain(self):
        for t in self.first.others():
            self.step1(t, False).wait_send()
            self.step3(t, False).wait_send()
        for t in self.second.others():
            self.step2(t, False).wait_send()


def pair(ref, z, y, step=1):
    a = ref[pl.ds(z, 3), pl.ds(y, 3)]
    b = ref[pl.ds(z, 3), pl.ds(y + step, 3)]
    rows = 9 * ref.shape[2]
    return jnp.concatenate([a.reshape(rows, ref.shape[3]), b.reshape(rows, ref.shape[3])], axis=1)


def silu_slope(value):
    sigma = 1.0 / (1.0 + jnp.exp(-value))
    return sigma * (1.0 + value * (1.0 - sigma))


def silu(value):
    return value / (1.0 + jnp.exp(-value))


def kernel(
    nz, ny, scale,
    feat_ref, cot_ref, wenc_hbm, wmid_hbm, wdec_hbm,
    decoded_ref, genc_ref, gmid_ref, gdec_ref,
    fh, ch, sh, ph, oh, bh,
    fx, cx, sx, px, ox, bx,
    wenc_ref, wmid_ref, wdec_ref, wsem, we_ref, wm_ref, ws_ref, wc_ref, wb_ref, wp_ref, turned,
    slope, bskip, bsum, boxed, skips, benc, dec_acc, enc_acc, mid_acc, dplane,
    a_mine, a_one, a_two, a_whole, b_mine, b_one, b_two, b_whole,
    fin, cin, dout, msend, mrecv, hsend, hrecv, as1, ar1, as2, ar2, as3, ar3, bs1, br1, bs2, br2, bs3, br3,
):
    gz, gy = lax.axis_index("gz"), lax.axis_index("gy")
    vz, vy = block(gz, gy)
    stays = (vz == gz) & (vy == gy)
    c1, depth, height, width = feat_ref.shape
    half = width // 2
    c2 = bsum.shape[1]
    chigh = height // 2
    grid = (vz, vy, nz, ny)
    fhalo, chalo, shalo, phalo, ohalo, bhalo = [
        Halo(ref, hsend, hrecv, n, grid) for n, ref in enumerate((fh, ch, sh, ph, oh, bh))
    ]
    near, core = gz // 2, lax.rem(gy, 2)
    chip = ny // 2 * lax.rem(gz, 2) + gy // 2
    column = Group(
        2 * ny,
        2 * chip + core,
        lambda t: (gz - lax.rem(gz, 2) + t // ny, lax.rem(t, ny)),
        [
            2 * lax.rem(chip + d, ny) + lax.rem(core + e, 2)
            for d, e in ((2, 0), (2, 1), (1, 0), (3, 0), (1, 1), (3, 1), (0, 1))
        ],
    )
    side = 4
    far = {0: 0, 1: 1, 2: 2, 3: 1}
    steps = sorted(((a, b) for a in range(side) for b in range(side)), key=lambda s: -far[s[0]] - far[s[1]])
    plane = Group(
        nz // 2,
        near,
        lambda t: (2 * t + lax.rem(gz, 2), gy),
        [
            side * lax.rem(near // side + a, side) + lax.rem(lax.rem(near, side) + b, side)
            for a, b in steps[:-1]
        ],
    )

    barrier = pltpu.get_barrier_semaphore()
    away = vz + 2 * lax.rem(vz, 2) - 1
    arrivals = column.size + plane.size - 2
    for b in (-1, 0, 1):
        near = (away >= 0) & (away < nz) & (vy + b >= 0) & (vy + b < ny)
        arrivals = arrivals + jnp.where(near, 1, 0)

        @pl.when(near)
        def _(b=b):
            pl.semaphore_signal(barrier, inc=1, device_id=place(away, vy + b), device_id_type=MESH)
    for group in (column, plane):
        for t in group.others():
            pl.semaphore_signal(barrier, inc=1, device_id=group.peer(t), device_id_type=MESH)

    weights = [
        pltpu.make_async_copy(src, dst, wsem.at[n])
        for n, (src, dst) in enumerate(
            ((wenc_hbm, wenc_ref), (wmid_hbm, wmid_ref), (wdec_hbm, wdec_ref))
        )
    ]
    for copy in weights:
        copy.start()
    target = place(gz, gy)
    moves = [
        [
            Move(src.at[:, z], dst.at[:, z], msend.at[n, z], mrecv.at[n, z], target, stays)
            for z in range(depth)
        ]
        for n, (src, dst) in enumerate(((feat_ref, fin), (cot_ref, cin)))
    ]
    to_cells = rows_to_cells(c1, height)

    def take(n, src, dst, halo):
        for z in range(depth):
            moves[n][z].wait_recv()
            own = src[:, z].astype(F32).reshape(c1 * height, width).astype(BF)
            own = dot(to_cells, own).astype(BF).reshape(height, c1, width)
            dst[1 + z, pl.ds(1, height)] = own
            halo.start((1, 0, 2) if z == 0 else (6, 5, 7, 3, 4))

    pl.semaphore_wait(barrier, arrivals)
    for listed in moves:
        for copy in listed:
            copy.start()
    for halo in (fhalo, chalo, shalo, phalo, ohalo, bhalo):
        halo.clear()
    a_mine[...] = jnp.zeros(a_mine.shape, BF)
    b_mine[...] = jnp.zeros(b_mine.shape, BF)
    boxed[...] = jnp.zeros(boxed.shape, BF)
    ox[...] = jnp.zeros(ox.shape, BF)
    bx[...] = jnp.zeros(bx.shape, BF)
    for copy in weights:
        copy.wait()
    prepare(wenc_ref, wmid_ref, wdec_ref, we_ref, wm_ref, ws_ref, wc_ref, wb_ref, wp_ref, turned)
    px[...] = jnp.zeros(px.shape, BF)
    dec_acc[...] = jnp.zeros(dec_acc.shape, F32)
    enc_acc[...] = jnp.zeros(enc_acc.shape, F32)
    mid_acc[...] = jnp.zeros(mid_acc.shape, F32)
    take(0, fin, fh, fhalo)
    take(1, cin, ch, chalo)

    def four(src, dst):
        spread = split_four(width)

        def body(z, carry):
            rows = src[z].reshape((height + 2) * c1, width)
            out = dot(rows, spread).astype(BF).reshape(height + 2, c1, 2 * width)
            for j in range(4):
                dst[z, :, j * c1 : (j + 1) * c1, :] = out[:, :, j * half : (j + 1) * half]
            return carry

        lax.fori_loop(0, depth + 2, body, 0)

    fhalo.arrived()
    four(fh, fx)

    def encode(yc, carry):
        pool = jnp.zeros((c1, half), F32)
        for z in range(depth):
            pre = dot(we_ref[...], pair(fx, z, 2 * yc))
            act = silu(pre).astype(BF)
            der = silu_slope(pre)
            for p in range(2):
                cell = act[:, p * half : (p + 1) * half]
                slope[z, 2 * yc + p] = der[:, p * half : (p + 1) * half]
                for q in range(2):
                    part = cell[q * c1 : (q + 1) * c1]
                    sh[1 + z, 1 + 2 * yc + p, :, q * half : (q + 1) * half] = part
                    skips[z, 2 * yc + p, q * c1 : (q + 1) * c1, :] = part
                    pool = pool + part.astype(F32)
        ph[1, 1 + yc] = (pool * 0.125).astype(BF)
        return carry

    lax.fori_loop(0, chigh, encode, 0)
    phalo.start()
    shalo.start()

    chalo.arrived()
    four(ch, cx)

    def backward(yc, carry):
        low = jnp.zeros((c2, half), F32)
        for z in range(depth):
            out = dot(wb_ref[...], pair(cx, z, 2 * yc))
            for p in range(2):
                for q in range(2):
                    part = out[q * (c1 + c2) : (q + 1) * (c1 + c2), p * half : (p + 1) * half]
                    low = low + part[:c2]
                    bskip[z, 2 * yc + p, q * c1 : (q + 1) * c1, :] = part[c2:]
        bsum[yc] = low
        return carry

    lax.fori_loop(0, chigh, backward, 0)

    def box(yc, carry):
        for w in range(3):
            low = cx[w, pl.ds(2 * yc, 4)].astype(F32) + cx[w + 1, pl.ds(2 * yc, 4)].astype(F32)
            for v in range(3):
                both = low[v] + low[v + 1]
                boxed[pl.ds((3 * w + v) * 3 * c1, 3 * c1), pl.ds(pl.multiple_of(yc * half, half), half)] = (
                    both[: 3 * c1] + both[c1:]
                ).astype(BF)
        return carry

    lax.fori_loop(0, chigh, box, 0)

    sides = shift_both(half)

    def three(src, dst):
        chans = src.shape[2]
        rows = src[...].reshape(src.shape[0] * src.shape[1] * chans, half)
        out = dot(rows, sides).astype(BF).reshape(src.shape[0], src.shape[1], chans, 2 * half)
        dst[:, :, 0:chans, :] = out[..., :half]
        dst[:, :, chans : 2 * chans, :] = src[...]
        dst[:, :, 2 * chans : 3 * chans, :] = out[..., half:]

    phalo.arrived()
    three(ph, px)
    for yc in range(0, chigh, 2):
        pre = dot(wm_ref[...], pair(px, 0, yc))
        for p in range(2):
            cell = pre[:, p * half : (p + 1) * half]
            act = silu(cell).astype(BF)
            oh[1, 1 + yc + p] = act
            bh[1, 1 + yc + p] = (silu_slope(cell) * bsum[yc + p]).astype(BF)
    bhalo.start()
    ohalo.start()

    own = jnp.concatenate([oh[1, 1 + yc] for yc in range(chigh)], axis=1)
    none = jnp.zeros_like(own)
    low = dot_nt(boxed[: 14 * c1], jnp.concatenate([own, none], axis=0)) + dot_nt(
        boxed[14 * c1 :], jnp.concatenate([none, own], axis=0)
    )
    a_mine[0:7] = low.astype(BF).reshape(7, 64, 128)

    for yc in range(0, chigh, 2):
        own = jnp.concatenate([bh[1, 1 + yc], bh[1, 2 + yc]], axis=1)
        mid_acc[...] += dot_nt(pair(px, 0, yc), jnp.concatenate([own, own], axis=0))

    def mid_rows(k):
        row = (k // 3) * 128 + (k % 3) * c1
        return mid_acc[row : row + c1, :]

    first = iota((c1, 128), 1) < c2
    for d in range(14):
        piece = jnp.where(first, mid_rows(d), mid_rows(d + 14)) if d < 13 else mid_rows(d)
        a_mine[7 + d // 2, (d % 2) * 32 : (d % 2 + 1) * 32, :] = piece.astype(BF)
    a_total = Total(plane, column, a_mine, a_one, a_two, a_whole, (as1, ar1, as2, ar2, as3, ar3))
    a_total.start1()

    def decoder_grad(yc, carry):
        for z in range(depth):
            own = jnp.concatenate([skips[z, 2 * yc], skips[z, 2 * yc + 1]], axis=1)
            dec_acc[...] += dot_nt(own, pair(cx, z, 2 * yc))
        return carry

    lax.fori_loop(0, chigh, decoder_grad, 0)

    def pack(acc, first):
        for kk in range(9):
            even = acc[0:c1, kk * 128 : (kk + 1) * 128]
            odd = acc[c1 : 2 * c1, kk * 128 : (kk + 1) * 128]
            piece = (even + pltpu.roll(odd, 128 - c1, 1)).astype(BF)
            for h in range(2):
                n = first + 2 * kk + h
                b_mine[n // 5, (n % 5) * 16 : (n % 5 + 1) * 16, :] = piece[h * 16 : (h + 1) * 16]

    pack(dec_acc, 18)

    bhalo.arrived()
    three(bh, bx)
    for yc in range(0, chigh, 2):
        pool = dot(wp_ref[...], pair(bx, 0, yc)) * 0.125
        for p in range(2):
            up = pool[:, p * half : (p + 1) * half]
            up = jnp.concatenate([up, up], axis=0)
            for z in range(depth):
                for r in range(2):
                    y = 2 * (yc + p) + r
                    benc[z, y] = (slope[z, y] * (bskip[z, y] + up)).astype(BF)

    def encoder_grad(yc, carry):
        for z in range(depth):
            own = jnp.concatenate([benc[z, 2 * yc], benc[z, 2 * yc + 1]], axis=1)
            enc_acc[...] += dot_nt(own, pair(fx, z, 2 * yc))
        return carry

    lax.fori_loop(0, chigh, encoder_grad, 0)
    pack(enc_acc, 0)
    b_total = Total(column, plane, b_mine, b_one, b_two, b_whole, (bs1, br1, bs2, br2, bs3, br3))
    b_total.start1()
    a_total.start2()

    shalo.arrived()
    turn = shift_parity(width)

    def four_skip(z, carry):
        rows = sh[z].reshape((height + 2) * c1, width)
        out = dot(rows, turn).astype(BF).reshape(height + 2, c1, width)
        sx[z, :, 0:c1, :] = out[:, :, :half]
        sx[z, :, c1 : 2 * c1, :] = sh[z, :, :, 0:half]
        sx[z, :, 2 * c1 : 3 * c1, :] = sh[z, :, :, half:width]
        sx[z, :, 3 * c1 : 4 * c1, :] = out[:, :, half:]
        return carry

    lax.fori_loop(0, depth + 2, four_skip, 0)
    ohalo.arrived()
    three(oh, ox)
    b_total.start2()
    a_total.start3()

    def decode(yc, carry):
        for z in range(depth):
            out = dot(ws_ref[...], pair(sx, z, 2 * yc))
            for p in range(2):
                field = ox[pl.ds(z, 2), pl.ds(yc + p, 2)].reshape(4 * 4 * c2, half)
                row = (out[:, p * half : (p + 1) * half] + dot(wc_ref[2 * z + p], field)).astype(BF)
                for q in range(2):
                    dplane[z, 2 * yc + p, :, q * half : (q + 1) * half] = row[q * c1 : (q + 1) * c1]
        return carry

    lax.fori_loop(0, chigh, decode, 0)
    to_rows = cells_to_rows(c1, height)
    merge = merge_parity(width)
    back = [
        Move(dout.at[:, z], decoded_ref.at[:, z], msend.at[2, z], mrecv.at[2, z], (vz, vy), stays)
        for z in range(depth)
    ]
    for z in range(depth):
        rows = dplane[z].reshape(height * c1, width)
        rows = dot(rows, merge).astype(BF)
        dout[:, z] = dot(to_rows, rows).reshape(c1, height, width).astype(BF)
        back[z].start()

    b_total.start3()
    a_total.finish()
    for r in range(27):
        half_of, n = r // 14, r % 14
        gdec_ref[26 - r, :, 0:c2] = a_whole[
            n // 2, (n % 2) * 32 : (n % 2 + 1) * 32, half_of * c2 : (half_of + 1) * c2
        ].astype(F32) * scale
    for k in range(27):
        half_of, n = k // 14, k % 14
        gmid_ref[k] = a_whole[
            7 + n // 2, (n % 2) * 32 : (n % 2 + 1) * 32, half_of * c2 : (half_of + 1) * c2
        ].astype(F32) * scale
    b_total.finish()

    def unpack(n):
        return b_whole[n // 5, (n % 5) * 16 : (n % 5 + 1) * 16, :].astype(F32) * scale

    for n in range(18):
        kk, h = n // 2, n % 2
        piece = unpack(n)
        for kx in range(3):
            genc_ref[3 * kk + kx, h * 16 : (h + 1) * 16, :] = piece[:, kx * 32 : (kx + 1) * 32]
    for kk in range(9):
        piece = jnp.concatenate([unpack(18 + 2 * kk), unpack(19 + 2 * kk)], axis=0).T
        for kx in range(3):
            gdec_ref[3 * (8 - kk) + 2 - kx, :, c2 : c2 + c1] = piece[kx * c1 : (kx + 1) * c1]

    for copy in back:
        copy.wait_recv()
    for copy in moves[0] + moves[1] + back:
        copy.wait_send()
    for halo in (fhalo, chalo, shalo, phalo, ohalo, bhalo):
        halo.sent()
    a_total.drain()
    b_total.drain()


def split_weights(w_ref, kx):
    return jnp.concatenate([w_ref[3 * kk + kx] for kk in range(9)], axis=0)


def fine_weights(w_ref, first, dst):
    outs, ins, n = w_ref.shape[1], w_ref.shape[2], dst.shape[1] // 36
    total = jnp.zeros((9 * outs, 8 * n), F32)
    for kx in range(3):
        r, c = iota((ins, 8 * n), 0), iota((ins, 8 * n), 1)
        px, jx, i = c // (4 * n), (c // n) % 4, c % n
        total = total + dot(split_weights(w_ref, kx), hot((jx == kx + px) & (r == first + i)))
    total = total.astype(BF)
    for kk in range(9):
        for p in range(2):
            dst[p * outs : (p + 1) * outs, kk * 4 * n : (kk + 1) * 4 * n] = total[
                kk * outs : (kk + 1) * outs, p * 4 * n : (p + 1) * 4 * n
            ]


def prepare(wenc_ref, wmid_ref, wdec_ref, we_ref, wm_ref, ws_ref, wc_ref, wb_ref, wp_ref, turned):
    c1, c2 = wmid_ref.shape[1:]
    fine_weights(wenc_ref, 0, we_ref)
    fine_weights(wdec_ref, c2, ws_ref)

    blank = jnp.zeros((c1, c2), BF)
    rows = [wmid_ref[3 * kk + kx] if kx < 3 else blank for kk in range(9) for kx in range(4)]
    pick = hot(iota((c2, c2), 0) == iota((c2, c2), 1))
    wm_ref[...] = dot_nt(pick, jnp.concatenate(rows, axis=0)).astype(BF)
    total = jnp.zeros((9 * c1, 4 * c2), F32)
    for kx in range(3):
        rows = jnp.concatenate([wmid_ref[26 - 3 * kk - kx] for kk in range(9)], axis=0)
        r, c = iota((c2, 4 * c2), 0), iota((c2, 4 * c2), 1)
        total = total + dot(rows, hot(c == kx * c2 + r))
    total = total.astype(BF)
    for kk in range(9):
        wp_ref[:, kk * 4 * c2 : (kk + 1) * 4 * c2] = total[kk * c1 : (kk + 1) * c1]

    total = jnp.zeros((9 * c1, 8 * c2), F32)
    for kx in range(3):
        r, c = iota((c1 + c2, 8 * c2), 0), iota((c1 + c2, 8 * c2), 1)
        px, slot, i = c // (4 * c2), (c // c2) % 4, c % c2
        wanted = (kx + px + 1) // 2
        total = total + dot(split_weights(wdec_ref, kx), hot((slot == wanted) & (r == i)))
    parts = [[[0], [1, 2]], [[0, 1], [2]]]
    for pz in range(2):
        for py in range(2):
            for cz in range(2):
                for cy in range(2):
                    part = sum(
                        total[(3 * kz + ky) * c1 : (3 * kz + ky + 1) * c1]
                        for kz in parts[pz][cz]
                        for ky in parts[py][cy]
                    ).astype(BF)
                    at = (2 * cz + cy) * 4 * c2
                    for p in range(2):
                        wc_ref[2 * pz + py, p * c1 : (p + 1) * c1, at : at + 4 * c2] = part[
                            :, p * 4 * c2 : (p + 1) * 4 * c2
                        ]

    turned[...] = jnp.zeros(turned.shape, BF)
    blank = jnp.zeros((c1, c1 + c2), BF)
    for kk in range(9):
        for p in range(2):
            for jx in range(4):
                kx = jx - p
                value = wdec_ref[26 - 3 * kk - kx] if 0 <= kx < 3 else blank
                row = kk * 4 * c1 + jx * c1
                turned[row : row + c1, p * 128 : p * 128 + c1 + c2] = value
    r, c = iota((2 * (c1 + c2), 256), 0), iota((2 * (c1 + c2), 256), 1)
    pick = hot(c == (r // (c1 + c2)) * 128 + r % (c1 + c2))
    wb_ref[...] = dot_nt(pick, turned[...]).astype(BF)


def local(features, w_enc, w_mid, w_dec, cotangent):
    nz, ny = lax.axis_size("gz"), lax.axis_size("gy")
    c1, depth, height, width = features.shape
    c2 = w_mid.shape[1]
    w_mid = w_mid.transpose(0, 2, 1)
    half, ch = width // 2, height // 2
    assert nz == 32 and ny == 4 and depth == 2 and c1 == 32 and c2 == 64 and half == 128
    scale = (depth * nz * height * ny * width) ** (-0.5)
    n1, n2 = nz // 2, 2 * ny
    vmem = pl.BlockSpec(memory_space=pltpu.VMEM)
    anywhere = pl.BlockSpec(memory_space=pl.ANY)
    dma = pltpu.SemaphoreType.DMA
    fine, coarse = (depth + 2, height + 2), (3, ch + 2)
    decoded, genc, gmid, gdec = pl.pallas_call(
        functools.partial(kernel, nz, ny, scale),
        out_shape=(
            jax.ShapeDtypeStruct(features.shape, BF),
            jax.ShapeDtypeStruct(w_enc.shape, F32),
            jax.ShapeDtypeStruct(w_mid.shape, F32),
            jax.ShapeDtypeStruct(w_dec.shape, F32),
        ),
        in_specs=[anywhere] * 5,
        out_specs=[anywhere] + [vmem] * 3,
        scratch_shapes=[
            pltpu.VMEM(fine + (c1, width), BF),
            pltpu.VMEM(fine + (c1, width), BF),
            pltpu.VMEM(fine + (c1, width), BF),
            pltpu.VMEM(coarse + (c1, half), BF),
            pltpu.VMEM(coarse + (c2, half), BF),
            pltpu.VMEM(coarse + (c2, half), BF),
            pltpu.VMEM(fine + (4 * c1, half), BF),
            pltpu.VMEM(fine + (4 * c1, half), BF),
            pltpu.VMEM(fine + (4 * c1, half), BF),
            pltpu.VMEM(coarse + (4 * c1, half), BF),
            pltpu.VMEM(coarse + (4 * c2, half), BF),
            pltpu.VMEM(coarse + (4 * c2, half), BF),
            pltpu.VMEM(w_enc.shape, BF),
            pltpu.VMEM(w_mid.shape, BF),
            pltpu.VMEM(w_dec.shape, BF),
            dma((3,)),
            pltpu.VMEM((2 * c1, 36 * c1), BF),
            pltpu.VMEM((c2, 36 * c1), BF),
            pltpu.VMEM((2 * c1, 36 * c1), BF),
            pltpu.VMEM((4, 2 * c1, 16 * c2), BF),
            pltpu.VMEM((2 * (c1 + c2), 36 * c1), BF),
            pltpu.VMEM((c1, 36 * c2), BF),
            pltpu.VMEM((36 * c1, 256), BF),
            pltpu.VMEM((depth, height, 2 * c1, half), F32),
            pltpu.VMEM((depth, height, 2 * c1, half), F32),
            pltpu.VMEM((ch, c2, half), F32),
            pltpu.VMEM((28 * c1, ch * half), BF),
            pltpu.VMEM((depth, height, 2 * c1, half), BF),
            pltpu.VMEM((depth, height, 2 * c1, half), BF),
            pltpu.VMEM((2 * c1, 9 * 128), F32),
            pltpu.VMEM((2 * c1, 9 * 128), F32),
            pltpu.VMEM((9 * 128, 128), F32),
            pltpu.VMEM((depth, height, c1, width), BF),
            pltpu.VMEM((n1, 64, 128), BF),
            pltpu.VMEM((n1, 64, 128), BF),
            pltpu.VMEM((n2, 64, 128), BF),
            pltpu.VMEM((n1, 64, 128), BF),
            pltpu.VMEM((n2, 80, 128), BF),
            pltpu.VMEM((n2, 80, 128), BF),
            pltpu.VMEM((n1, 80, 128), BF),
            pltpu.VMEM((n2, 80, 128), BF),
            pltpu.VMEM(features.shape, BF),
            pltpu.VMEM(features.shape, BF),
            pltpu.VMEM(features.shape, BF),
            dma((3, 2)), dma((3, 2)), dma((6, 8)), dma((6, 8)),
            dma((n1,)), dma((n1,)), dma((n2,)), dma((n2,)), dma((n1,)), dma((n1,)),
            dma((n2,)), dma((n2,)), dma((n1,)), dma((n1,)), dma((n2,)), dma((n2,)),
        ],
        compiler_params=pltpu.CompilerParams(
            collective_id=0, has_side_effects=True, vmem_limit_bytes=60 * 2**20
        ),
    )(features, cotangent, w_enc, w_mid, w_dec)
    return decoded, genc, gmid.transpose(0, 2, 1), gdec


def solution(mesh):
    placed = (P(None, "gz", "gy", None), P(), P(), P(), P(None, "gz", "gy", None))
    return jax.shard_map(
        local,
        mesh=mesh,
        in_specs=placed,
        out_specs=(P(None, "gz", "gy", None), P(), P(), P()),
        check_vma=False,
    )
```

```python
import functools

import jax
import jax.numpy as jnp
from jax import lax
from jax.experimental import pallas as pl
from jax.experimental.pallas import tpu as pltpu
from jax.sharding import PartitionSpec as P

MESH = pl.DeviceIdType.MESH
BF = jnp.bfloat16
F32 = jnp.float32
DIRECTIONS = [(a, b) for a in (-1, 0, 1) for b in (-1, 0, 1) if (a, b) != (0, 0)]


def iota(shape, dim):
    return lax.broadcasted_iota(jnp.int32, shape, dim)


def hot(mask):
    return jnp.where(mask, 1.0, 0.0).astype(BF)


def dot(a, b):
    return jnp.dot(a, b, preferred_element_type=F32)


def dot_nt(a, b):
    return lax.dot_general(a, b, (((1,), (1,)), ((), ())), preferred_element_type=F32)


def rows_to_cells(chans, height):
    n = chans * height
    r, s = iota((n, n), 0), iota((n, n), 1)
    return hot(s == (r % chans) * height + r // chans)


def cells_to_rows(chans, height):
    n = chans * height
    r, s = iota((n, n), 0), iota((n, n), 1)
    return hot(r == (s % chans) * height + s // chans)


def split_four(width):
    half = width // 2
    r, s = iota((width, 2 * width), 0), iota((width, 2 * width), 1)
    return hot(r == 2 * (s % half) - 1 + s // half)


def shift_parity(width):
    half = width // 2
    r, s = iota((width, width), 0), iota((width, width), 1)
    c = s % half
    first = (s < half) & (c > 0) & (r == half + c - 1)
    second = (s >= half) & (c < half - 1) & (r == c + 1)
    return hot(first | second)


def shift_both(half):
    r, s = iota((half, 2 * half), 0), iota((half, 2 * half), 1)
    return hot(((s < half) & (r == s - 1)) | ((s >= half) & (r == s - half + 1)))


def merge_parity(width):
    half = width // 2
    r, s = iota((width, width), 0), iota((width, width), 1)
    return hot(s == 2 * (r % half) + r // half)


def place(z, y):
    return (z - lax.rem(z, 2) + y // 2, 2 * lax.rem(y, 2) + lax.rem(z, 2))


def block(gz, gy):
    return gz - lax.rem(gz, 2) + lax.rem(gy, 2), 2 * lax.rem(gz, 2) + gy // 2


class Move:
    def __init__(self, src, dst, send, recv, peer, stays):
        self.src, self.dst, self.send, self.recv = src, dst, send, recv
        self.peer, self.stays = peer, stays

    def remote(self):
        return pltpu.make_async_remote_copy(
            src_ref=self.src, dst_ref=self.dst, send_sem=self.send, recv_sem=self.recv,
            device_id=self.peer, device_id_type=MESH,
        )

    def either(self, near, far):
        pl.when(self.stays)(lambda: near(pltpu.make_async_copy(self.src, self.dst, self.recv)))
        pl.when(jnp.logical_not(self.stays))(lambda: far(self.remote()))

    def start(self):
        self.either(lambda c: c.start(), lambda c: c.start())

    def wait_recv(self):
        self.either(lambda c: c.wait(), lambda c: c.wait_recv())

    def wait_send(self):
        pl.when(jnp.logical_not(self.stays))(lambda: self.remote().wait_send())


class Halo:
    def __init__(self, ref, send, recv, number, grid):
        self.ref, self.send, self.recv, self.number = ref, send, recv, number
        self.gz, self.gy, self.nz, self.ny = grid
        self.depth, self.height = ref.shape[0] - 2, ref.shape[1] - 2

    def exists(self, a, b):
        checks = []
        if a:
            checks.append(self.gz > 0 if a < 0 else self.gz < self.nz - 1)
        if b:
            checks.append(self.gy > 0 if b < 0 else self.gy < self.ny - 1)
        return functools.reduce(jnp.logical_and, checks)

    def source(self, d, n):
        return {-1: pl.ds(1, 1), 0: pl.ds(1, n), 1: pl.ds(n, 1)}[d]

    def target(self, d, n):
        return {-1: pl.ds(n + 1, 1), 0: pl.ds(1, n), 1: pl.ds(0, 1)}[d]

    def copy(self, i):
        a, b = DIRECTIONS[i]
        peer = place(lax.rem(self.gz + a + self.nz, self.nz), lax.rem(self.gy + b + self.ny, self.ny))
        return pltpu.make_async_remote_copy(
            src_ref=self.ref.at[self.source(a, self.depth), self.source(b, self.height)],
            dst_ref=self.ref.at[self.target(a, self.depth), self.target(b, self.height)],
            send_sem=self.send.at[self.number, i],
            recv_sem=self.recv.at[self.number, i],
            device_id=peer,
            device_id_type=MESH,
        )

    def start(self, listed=(1, 6, 3, 4, 0, 2, 5, 7)):
        for i in listed:
            pl.when(self.exists(*DIRECTIONS[i]))(lambda i=i: self.copy(i).start())

    def clear(self):
        for i, (a, b) in enumerate(DIRECTIONS):
            @pl.when(jnp.logical_not(self.exists(-a, -b)))
            def _(a=a, b=b):
                part = self.ref.at[self.target(a, self.depth), self.target(b, self.height)]
                part[...] = jnp.zeros(part.shape, part.dtype)

    def arrived(self):
        for i, (a, b) in enumerate(DIRECTIONS):
            pl.when(self.exists(-a, -b))(lambda i=i: self.copy(i).wait_recv())

    def sent(self):
        for i, (a, b) in enumerate(DIRECTIONS):
            pl.when(self.exists(a, b))(lambda i=i: self.copy(i).wait_send())


class Group:
    def __init__(self, size, me, peer, listed):
        self.size, self.me, self.peer, self.listed = size, me, peer, listed

    def others(self):
        return self.listed


class Total:
    def __init__(self, first, second, mine, one, two, whole, sems):
        self.first, self.second = first, second
        self.mine, self.one, self.two, self.whole = mine, one, two, whole
        self.send1, self.recv1, self.send2, self.recv2, self.send3, self.recv3 = sems

    def copy(self, src, dst, send, recv, slot, peer):
        return pltpu.make_async_remote_copy(
            src_ref=src, dst_ref=dst, send_sem=send, recv_sem=recv,
            device_id=peer, device_id_type=MESH,
        )

    def step1(self, t, incoming):
        g = self.first
        slot = t if incoming else g.me
        return self.copy(self.mine.at[t], self.one.at[slot], self.send1.at[t], self.recv1.at[slot], slot, g.peer(t))

    def step2(self, t, incoming):
        g = self.second
        slot = t if incoming else g.me
        return self.copy(self.two.at[g.me], self.two.at[slot], self.send2.at[t], self.recv2.at[slot], slot, g.peer(t))

    def step3(self, t, incoming):
        g = self.first
        slot = t if incoming else g.me
        return self.copy(self.whole.at[g.me], self.whole.at[slot], self.send3.at[t], self.recv3.at[slot], slot, g.peer(t))

    def start1(self):
        for t in self.first.others():
            self.step1(t, False).start()

    def start2(self):
        total = self.mine[self.first.me].astype(F32)
        for t in self.first.others():
            self.step1(t, True).wait_recv()
            total = total + self.one[t].astype(F32)
        self.two[self.second.me] = total.astype(BF)
        for t in self.second.others():
            self.step2(t, False).start()

    def start3(self):
        for t in self.second.others():
            self.step2(t, True).wait_recv()
        total = self.two[0].astype(F32)
        for t in range(1, self.second.size):
            total = total + self.two[t].astype(F32)
        self.whole[self.first.me] = total.astype(BF)
        for t in self.first.others():
            self.step3(t, False).start()

    def finish(self):
        for t in self.first.others():
            self.step3(t, True).wait_recv()

    def drain(self):
        for t in self.first.others():
            self.step1(t, False).wait_send()
            self.step3(t, False).wait_send()
        for t in self.second.others():
            self.step2(t, False).wait_send()


def pair(ref, z, y, step=1):
    a = ref[pl.ds(z, 3), pl.ds(y, 3)]
    b = ref[pl.ds(z, 3), pl.ds(y + step, 3)]
    rows = 9 * ref.shape[2]
    return jnp.concatenate([a.reshape(rows, ref.shape[3]), b.reshape(rows, ref.shape[3])], axis=1)


def silu_slope(value):
    sigma = 1.0 / (1.0 + jnp.exp(-value))
    return sigma * (1.0 + value * (1.0 - sigma))


def silu(value):
    return value / (1.0 + jnp.exp(-value))


def kernel(
    nz, ny,
    feat_ref, cot_ref, wenc_hbm, wmid_hbm, wdec_hbm,
    decoded_ref, a_whole, b_whole,
    fh, ch, sh, ph, oh, bh,
    fx, cx, sx, px, ox, bx,
    wenc_ref, wmid_ref, wdec_ref, wsem, we_ref, wm_ref, ws_ref, wc_ref, wb_ref, wp_ref, turned,
    slope, bskip, bsum, boxed, skips, benc, dec_acc, enc_acc, mid_acc, dplane,
    a_mine, a_one, a_two, b_mine, b_one, b_two,
    fin, cin, dout, msend, mrecv, hsend, hrecv, as1, ar1, as2, ar2, as3, ar3, bs1, br1, bs2, br2, bs3, br3,
):
    gz, gy = lax.axis_index("gz"), lax.axis_index("gy")
    vz, vy = block(gz, gy)
    stays = (vz == gz) & (vy == gy)
    c1, depth, height, width = feat_ref.shape
    half = width // 2
    c2 = bsum.shape[1]
    chigh = height // 2
    grid = (vz, vy, nz, ny)
    fhalo, chalo, shalo, phalo, ohalo, bhalo = [
        Halo(ref, hsend, hrecv, n, grid) for n, ref in enumerate((fh, ch, sh, ph, oh, bh))
    ]
    near, core = gz // 2, lax.rem(gy, 2)
    chip = ny // 2 * lax.rem(gz, 2) + gy // 2
    column = Group(
        2 * ny,
        2 * chip + core,
        lambda t: (gz - lax.rem(gz, 2) + t // ny, lax.rem(t, ny)),
        [
            2 * lax.rem(chip + d, ny) + lax.rem(core + e, 2)
            for d, e in ((2, 0), (2, 1), (1, 0), (3, 0), (1, 1), (3, 1), (0, 1))
        ],
    )
    side = 4
    far = {0: 0, 1: 1, 2: 2, 3: 1}
    steps = sorted(((a, b) for a in range(side) for b in range(side)), key=lambda s: -far[s[0]] - far[s[1]])
    plane = Group(
        nz // 2,
        near,
        lambda t: (2 * t + lax.rem(gz, 2), gy),
        [
            side * lax.rem(near // side + a, side) + lax.rem(lax.rem(near, side) + b, side)
            for a, b in steps[:-1]
        ],
    )

    barrier = pltpu.get_barrier_semaphore()
    away = vz + 2 * lax.rem(vz, 2) - 1
    arrivals = column.size + plane.size - 2
    for b in (-1, 0, 1):
        near = (away >= 0) & (away < nz) & (vy + b >= 0) & (vy + b < ny)
        arrivals = arrivals + jnp.where(near, 1, 0)

        @pl.when(near)
        def _(b=b):
            pl.semaphore_signal(barrier, inc=1, device_id=place(away, vy + b), device_id_type=MESH)
    for group in (column, plane):
        for t in group.others():
            pl.semaphore_signal(barrier, inc=1, device_id=group.peer(t), device_id_type=MESH)

    weights = [
        pltpu.make_async_copy(src, dst, wsem.at[n])
        for n, (src, dst) in enumerate(
            ((wenc_hbm, wenc_ref), (wmid_hbm, wmid_ref), (wdec_hbm, wdec_ref))
        )
    ]
    for copy in weights:
        copy.start()
    target = place(gz, gy)
    moves = [
        [
            Move(src.at[:, z], dst.at[:, z], msend.at[n, z], mrecv.at[n, z], target, stays)
            for z in range(depth)
        ]
        for n, (src, dst) in enumerate(((feat_ref, fin), (cot_ref, cin)))
    ]
    to_cells = rows_to_cells(c1, height)

    def take(n, src, dst, halo):
        for z in range(depth):
            moves[n][z].wait_recv()
            own = src[:, z].astype(F32).reshape(c1 * height, width).astype(BF)
            own = dot(to_cells, own).astype(BF).reshape(height, c1, width)
            dst[1 + z, pl.ds(1, height)] = own
            halo.start((1, 0, 2) if z == 0 else (6, 5, 7, 3, 4))

    pl.semaphore_wait(barrier, arrivals)
    for listed in moves:
        for copy in listed:
            copy.start()
    for halo in (fhalo, chalo, shalo, phalo, ohalo, bhalo):
        halo.clear()
    a_mine[...] = jnp.zeros(a_mine.shape, BF)
    b_mine[...] = jnp.zeros(b_mine.shape, BF)
    boxed[...] = jnp.zeros(boxed.shape, BF)
    ox[...] = jnp.zeros(ox.shape, BF)
    bx[...] = jnp.zeros(bx.shape, BF)
    for copy in weights:
        copy.wait()
    prepare(wenc_ref, wmid_ref, wdec_ref, we_ref, wm_ref, ws_ref, wc_ref, wb_ref, wp_ref, turned)
    px[...] = jnp.zeros(px.shape, BF)
    dec_acc[...] = jnp.zeros(dec_acc.shape, F32)
    enc_acc[...] = jnp.zeros(enc_acc.shape, F32)
    mid_acc[...] = jnp.zeros(mid_acc.shape, F32)
    take(0, fin, fh, fhalo)
    take(1, cin, ch, chalo)

    def four(src, dst):
        spread = split_four(width)

        def body(z, carry):
            rows = src[z].reshape((height + 2) * c1, width)
            out = dot(rows, spread).astype(BF).reshape(height + 2, c1, 2 * width)
            for j in range(4):
                dst[z, :, j * c1 : (j + 1) * c1, :] = out[:, :, j * half : (j + 1) * half]
            return carry

        lax.fori_loop(0, depth + 2, body, 0)

    fhalo.arrived()
    four(fh, fx)

    def encode(yc, carry):
        pool = jnp.zeros((c1, half), F32)
        for z in range(depth):
            pre = dot(we_ref[...], pair(fx, z, 2 * yc))
            act = silu(pre).astype(BF)
            der = silu_slope(pre)
            for p in range(2):
                cell = act[:, p * half : (p + 1) * half]
                slope[z, 2 * yc + p] = der[:, p * half : (p + 1) * half]
                for q in range(2):
                    part = cell[q * c1 : (q + 1) * c1]
                    sh[1 + z, 1 + 2 * yc + p, :, q * half : (q + 1) * half] = part
                    skips[z, 2 * yc + p, q * c1 : (q + 1) * c1, :] = part
                    pool = pool + part.astype(F32)
        ph[1, 1 + yc] = (pool * 0.125).astype(BF)
        return carry

    lax.fori_loop(0, chigh, encode, 0)
    phalo.start()
    shalo.start()

    chalo.arrived()
    four(ch, cx)

    def backward(yc, carry):
        low = jnp.zeros((c2, half), F32)
        for z in range(depth):
            out = dot(wb_ref[...], pair(cx, z, 2 * yc))
            for p in range(2):
                for q in range(2):
                    part = out[q * (c1 + c2) : (q + 1) * (c1 + c2), p * half : (p + 1) * half]
                    low = low + part[:c2]
                    bskip[z, 2 * yc + p, q * c1 : (q + 1) * c1, :] = part[c2:]
        bsum[yc] = low
        return carry

    lax.fori_loop(0, chigh, backward, 0)

    def box(yc, carry):
        for w in range(3):
            low = cx[w, pl.ds(2 * yc, 4)].astype(F32) + cx[w + 1, pl.ds(2 * yc, 4)].astype(F32)
            for v in range(3):
                both = low[v] + low[v + 1]
                boxed[pl.ds((3 * w + v) * 3 * c1, 3 * c1), pl.ds(pl.multiple_of(yc * half, half), half)] = (
                    both[: 3 * c1] + both[c1:]
                ).astype(BF)
        return carry

    lax.fori_loop(0, chigh, box, 0)

    def store(dst, n, piece):
        each = dst.shape[1] // 16
        dst[n // each, (n % each) * 16 : (n % each + 1) * 16, :] = piece

    def decoder_grad(yc, carry):
        for z in range(depth):
            own = jnp.concatenate([skips[z, 2 * yc], skips[z, 2 * yc + 1]], axis=1)
            dec_acc[...] += dot_nt(own, pair(cx, z, 2 * yc))
        return carry

    lax.fori_loop(0, chigh, decoder_grad, 0)

    def pack(acc, dst, first):
        for kk in range(9):
            even = acc[0:c1, kk * 128 : (kk + 1) * 128]
            odd = acc[c1 : 2 * c1, kk * 128 : (kk + 1) * 128]
            piece = (even + pltpu.roll(odd, 128 - c1, 1)).astype(BF)
            for h in range(2):
                store(dst, first + 2 * kk + h, piece[h * 16 : (h + 1) * 16])

    pack(dec_acc, a_mine, 56)

    sides = shift_both(half)

    def three(src, dst):
        chans = src.shape[2]
        rows = src[...].reshape(src.shape[0] * src.shape[1] * chans, half)
        out = dot(rows, sides).astype(BF).reshape(src.shape[0], src.shape[1], chans, 2 * half)
        dst[:, :, 0:chans, :] = out[..., :half]
        dst[:, :, chans : 2 * chans, :] = src[...]
        dst[:, :, 2 * chans : 3 * chans, :] = out[..., half:]

    phalo.arrived()
    three(ph, px)
    for yc in range(0, chigh, 2):
        pre = dot(wm_ref[...], pair(px, 0, yc))
        for p in range(2):
            cell = pre[:, p * half : (p + 1) * half]
            act = silu(cell).astype(BF)
            oh[1, 1 + yc + p] = act
            bh[1, 1 + yc + p] = (silu_slope(cell) * bsum[yc + p]).astype(BF)
    bhalo.start()
    ohalo.start()

    own = jnp.concatenate([oh[1, 1 + yc] for yc in range(chigh)], axis=1)
    none = jnp.zeros_like(own)
    low = dot_nt(boxed[: 14 * c1], jnp.concatenate([own, none], axis=0)) + dot_nt(
        boxed[14 * c1 :], jnp.concatenate([none, own], axis=0)
    )
    low = low.astype(BF)
    for n in range(28):
        store(a_mine, n, low[n * 16 : (n + 1) * 16])

    for yc in range(0, chigh, 2):
        own = jnp.concatenate([bh[1, 1 + yc], bh[1, 2 + yc]], axis=1)
        mid_acc[...] += dot_nt(pair(px, 0, yc), jnp.concatenate([own, own], axis=0))

    def mid_rows(k):
        row = (k // 3) * 128 + (k % 3) * c1
        return mid_acc[row : row + c1, :]

    first = iota((c1, 128), 1) < c2
    for d in range(14):
        piece = jnp.where(first, mid_rows(d), mid_rows(d + 14)) if d < 13 else mid_rows(d)
        piece = piece.astype(BF)
        for h in range(2):
            store(a_mine, 28 + 2 * d + h, piece[h * 16 : (h + 1) * 16])
    a_total = Total(plane, column, a_mine, a_one, a_two, a_whole, (as1, ar1, as2, ar2, as3, ar3))
    a_total.start1()

    bhalo.arrived()
    three(bh, bx)
    for yc in range(0, chigh, 2):
        pool = dot(wp_ref[...], pair(bx, 0, yc)) * 0.125
        for p in range(2):
            up = pool[:, p * half : (p + 1) * half]
            up = jnp.concatenate([up, up], axis=0)
            for z in range(depth):
                for r in range(2):
                    y = 2 * (yc + p) + r
                    benc[z, y] = (slope[z, y] * (bskip[z, y] + up)).astype(BF)

    def encoder_grad(yc, carry):
        for z in range(depth):
            own = jnp.concatenate([benc[z, 2 * yc], benc[z, 2 * yc + 1]], axis=1)
            enc_acc[...] += dot_nt(own, pair(fx, z, 2 * yc))
        return carry

    lax.fori_loop(0, chigh, encoder_grad, 0)
    pack(enc_acc, b_mine, 0)
    b_total = Total(column, plane, b_mine, b_one, b_two, b_whole, (bs1, br1, bs2, br2, bs3, br3))
    b_total.start1()
    a_total.start2()

    shalo.arrived()
    turn = shift_parity(width)

    def four_skip(z, carry):
        rows = sh[z].reshape((height + 2) * c1, width)
        out = dot(rows, turn).astype(BF).reshape(height + 2, c1, width)
        sx[z, :, 0:c1, :] = out[:, :, :half]
        sx[z, :, c1 : 2 * c1, :] = sh[z, :, :, 0:half]
        sx[z, :, 2 * c1 : 3 * c1, :] = sh[z, :, :, half:width]
        sx[z, :, 3 * c1 : 4 * c1, :] = out[:, :, half:]
        return carry

    lax.fori_loop(0, depth + 2, four_skip, 0)
    ohalo.arrived()
    three(oh, ox)
    b_total.start2()
    a_total.start3()

    def decode(yc, carry):
        for z in range(depth):
            out = dot(ws_ref[...], pair(sx, z, 2 * yc))
            for p in range(2):
                field = ox[pl.ds(z, 2), pl.ds(yc + p, 2)].reshape(4 * 4 * c2, half)
                row = (out[:, p * half : (p + 1) * half] + dot(wc_ref[2 * z + p], field)).astype(BF)
                for q in range(2):
                    dplane[z, 2 * yc + p, :, q * half : (q + 1) * half] = row[q * c1 : (q + 1) * c1]
        return carry

    lax.fori_loop(0, chigh, decode, 0)
    to_rows = cells_to_rows(c1, height)
    merge = merge_parity(width)
    back = [
        Move(dout.at[:, z], decoded_ref.at[:, z], msend.at[2, z], mrecv.at[2, z], (vz, vy), stays)
        for z in range(depth)
    ]
    for z in range(depth):
        rows = dplane[z].reshape(height * c1, width)
        rows = dot(rows, merge).astype(BF)
        dout[:, z] = dot(to_rows, rows).reshape(c1, height, width).astype(BF)
        back[z].start()

    b_total.start3()
    a_total.finish()
    b_total.finish()
    for copy in back:
        copy.wait_recv()
    for copy in moves[0] + moves[1] + back:
        copy.wait_send()
    for halo in (fhalo, chalo, shalo, phalo, ohalo, bhalo):
        halo.sent()
    a_total.drain()
    b_total.drain()


def results(
    scale, moved_hbm, a_hbm, b_hbm, decoded_ref, genc_ref, gmid_ref, gdec_ref, moved_ref, a_ref, b_ref, sem
):
    copies = [
        pltpu.make_async_copy(src, dst, sem.at[n])
        for n, (src, dst) in enumerate(((a_hbm, a_ref), (b_hbm, b_ref), (moved_hbm, moved_ref)))
    ]
    for copy in copies:
        copy.start()
    c1, c2 = genc_ref.shape[1], gmid_ref.shape[2]

    def load(src, n):
        each = src.shape[1] // 16
        return src[n // each, (n % each) * 16 : (n % each + 1) * 16, :].astype(F32) * scale

    def both(src, n):
        return jnp.concatenate([load(src, n), load(src, n + 1)], axis=0)

    copies[2].wait()
    out = pltpu.make_async_copy(moved_ref, decoded_ref, sem.at[3])
    out.start()
    copies[0].wait()
    copies[1].wait()
    for d in range(14):
        low, mid = both(a_ref, 2 * d), both(a_ref, 28 + 2 * d)
        for h in range(2 if d < 13 else 1):
            gdec_ref[26 - d - 14 * h, :, 0:c2] = low[:, h * c2 : (h + 1) * c2]
            gmid_ref[d + 14 * h] = mid[:, h * c2 : (h + 1) * c2]
    for kk in range(9):
        skip, enc = both(a_ref, 56 + 2 * kk).T, both(b_ref, 2 * kk)
        for kx in range(3):
            gdec_ref[3 * (8 - kk) + 2 - kx, :, c2 : c2 + c1] = skip[kx * c1 : (kx + 1) * c1]
            genc_ref[3 * kk + kx] = enc[:, kx * c1 : (kx + 1) * c1]
    out.wait()


def split_weights(w_ref, kx):
    return jnp.concatenate([w_ref[3 * kk + kx] for kk in range(9)], axis=0)


def fine_weights(w_ref, first, dst):
    outs, ins, n = w_ref.shape[1], w_ref.shape[2], dst.shape[1] // 36
    total = jnp.zeros((9 * outs, 8 * n), F32)
    for kx in range(3):
        r, c = iota((ins, 8 * n), 0), iota((ins, 8 * n), 1)
        px, jx, i = c // (4 * n), (c // n) % 4, c % n
        total = total + dot(split_weights(w_ref, kx), hot((jx == kx + px) & (r == first + i)))
    total = total.astype(BF)
    for kk in range(9):
        for p in range(2):
            dst[p * outs : (p + 1) * outs, kk * 4 * n : (kk + 1) * 4 * n] = total[
                kk * outs : (kk + 1) * outs, p * 4 * n : (p + 1) * 4 * n
            ]


def prepare(wenc_ref, wmid_ref, wdec_ref, we_ref, wm_ref, ws_ref, wc_ref, wb_ref, wp_ref, turned):
    c1, c2 = wmid_ref.shape[1:]
    fine_weights(wenc_ref, 0, we_ref)
    fine_weights(wdec_ref, c2, ws_ref)

    blank = jnp.zeros((c1, c2), BF)
    rows = [wmid_ref[3 * kk + kx] if kx < 3 else blank for kk in range(9) for kx in range(4)]
    pick = hot(iota((c2, c2), 0) == iota((c2, c2), 1))
    wm_ref[...] = dot_nt(pick, jnp.concatenate(rows, axis=0)).astype(BF)
    total = jnp.zeros((9 * c1, 4 * c2), F32)
    for kx in range(3):
        rows = jnp.concatenate([wmid_ref[26 - 3 * kk - kx] for kk in range(9)], axis=0)
        r, c = iota((c2, 4 * c2), 0), iota((c2, 4 * c2), 1)
        total = total + dot(rows, hot(c == kx * c2 + r))
    total = total.astype(BF)
    for kk in range(9):
        wp_ref[:, kk * 4 * c2 : (kk + 1) * 4 * c2] = total[kk * c1 : (kk + 1) * c1]

    total = jnp.zeros((9 * c1, 8 * c2), F32)
    for kx in range(3):
        r, c = iota((c1 + c2, 8 * c2), 0), iota((c1 + c2, 8 * c2), 1)
        px, slot, i = c // (4 * c2), (c // c2) % 4, c % c2
        wanted = (kx + px + 1) // 2
        total = total + dot(split_weights(wdec_ref, kx), hot((slot == wanted) & (r == i)))
    parts = [[[0], [1, 2]], [[0, 1], [2]]]
    for pz in range(2):
        for py in range(2):
            for cz in range(2):
                for cy in range(2):
                    part = sum(
                        total[(3 * kz + ky) * c1 : (3 * kz + ky + 1) * c1]
                        for kz in parts[pz][cz]
                        for ky in parts[py][cy]
                    ).astype(BF)
                    at = (2 * cz + cy) * 4 * c2
                    for p in range(2):
                        wc_ref[2 * pz + py, p * c1 : (p + 1) * c1, at : at + 4 * c2] = part[
                            :, p * 4 * c2 : (p + 1) * 4 * c2
                        ]

    turned[...] = jnp.zeros(turned.shape, BF)
    blank = jnp.zeros((c1, c1 + c2), BF)
    for kk in range(9):
        for p in range(2):
            for jx in range(4):
                kx = jx - p
                value = wdec_ref[26 - 3 * kk - kx] if 0 <= kx < 3 else blank
                row = kk * 4 * c1 + jx * c1
                turned[row : row + c1, p * 128 : p * 128 + c1 + c2] = value
    r, c = iota((2 * (c1 + c2), 256), 0), iota((2 * (c1 + c2), 256), 1)
    pick = hot(c == (r // (c1 + c2)) * 128 + r % (c1 + c2))
    wb_ref[...] = dot_nt(pick, turned[...]).astype(BF)


def local(features, w_enc, w_mid, w_dec, cotangent):
    nz, ny = lax.axis_size("gz"), lax.axis_size("gy")
    c1, depth, height, width = features.shape
    c2 = w_mid.shape[1]
    w_mid = w_mid.transpose(0, 2, 1)
    half, ch = width // 2, height // 2
    assert nz == 32 and ny == 4 and depth == 2 and c1 == 32 and c2 == 64 and half == 128
    scale = (depth * nz * height * ny * width) ** (-0.5)
    n1, n2 = nz // 2, 2 * ny
    vmem = pl.BlockSpec(memory_space=pltpu.VMEM)
    anywhere = pl.BlockSpec(memory_space=pl.ANY)
    dma = pltpu.SemaphoreType.DMA
    fine, coarse = (depth + 2, height + 2), (3, ch + 2)
    moved, a_sum, b_sum = pl.pallas_call(
        functools.partial(kernel, nz, ny),
        out_shape=(
            jax.ShapeDtypeStruct(features.shape, BF),
            jax.ShapeDtypeStruct((n1, 80, 128), BF),
            jax.ShapeDtypeStruct((n2, 48, 128), BF),
        ),
        in_specs=[anywhere] * 5,
        out_specs=[anywhere] + [vmem] * 2,
        scratch_shapes=[
            pltpu.VMEM(fine + (c1, width), BF),
            pltpu.VMEM(fine + (c1, width), BF),
            pltpu.VMEM(fine + (c1, width), BF),
            pltpu.VMEM(coarse + (c1, half), BF),
            pltpu.VMEM(coarse + (c2, half), BF),
            pltpu.VMEM(coarse + (c2, half), BF),
            pltpu.VMEM(fine + (4 * c1, half), BF),
            pltpu.VMEM(fine + (4 * c1, half), BF),
            pltpu.VMEM(fine + (4 * c1, half), BF),
            pltpu.VMEM(coarse + (4 * c1, half), BF),
            pltpu.VMEM(coarse + (4 * c2, half), BF),
            pltpu.VMEM(coarse + (4 * c2, half), BF),
            pltpu.VMEM(w_enc.shape, BF),
            pltpu.VMEM(w_mid.shape, BF),
            pltpu.VMEM(w_dec.shape, BF),
            dma((3,)),
            pltpu.VMEM((2 * c1, 36 * c1), BF),
            pltpu.VMEM((c2, 36 * c1), BF),
            pltpu.VMEM((2 * c1, 36 * c1), BF),
            pltpu.VMEM((4, 2 * c1, 16 * c2), BF),
            pltpu.VMEM((2 * (c1 + c2), 36 * c1), BF),
            pltpu.VMEM((c1, 36 * c2), BF),
            pltpu.VMEM((36 * c1, 256), BF),
            pltpu.VMEM((depth, height, 2 * c1, half), F32),
            pltpu.VMEM((depth, height, 2 * c1, half), F32),
            pltpu.VMEM((ch, c2, half), F32),
            pltpu.VMEM((28 * c1, ch * half), BF),
            pltpu.VMEM((depth, height, 2 * c1, half), BF),
            pltpu.VMEM((depth, height, 2 * c1, half), BF),
            pltpu.VMEM((2 * c1, 9 * 128), F32),
            pltpu.VMEM((2 * c1, 9 * 128), F32),
            pltpu.VMEM((9 * 128, 128), F32),
            pltpu.VMEM((depth, height, c1, width), BF),
            pltpu.VMEM((n1, 80, 128), BF),
            pltpu.VMEM((n1, 80, 128), BF),
            pltpu.VMEM((n2, 80, 128), BF),
            pltpu.VMEM((n2, 48, 128), BF),
            pltpu.VMEM((n2, 48, 128), BF),
            pltpu.VMEM((n1, 48, 128), BF),
            pltpu.VMEM(features.shape, BF),
            pltpu.VMEM(features.shape, BF),
            pltpu.VMEM(features.shape, BF),
            dma((3, 2)), dma((3, 2)), dma((6, 8)), dma((6, 8)),
            dma((n1,)), dma((n1,)), dma((n2,)), dma((n2,)), dma((n1,)), dma((n1,)),
            dma((n2,)), dma((n2,)), dma((n1,)), dma((n1,)), dma((n2,)), dma((n2,)),
        ],
        compiler_params=pltpu.CompilerParams(
            collective_id=0, has_side_effects=True, vmem_limit_bytes=60 * 2**20
        ),
    )(features, cotangent, w_enc, w_mid, w_dec)
    decoded, genc, gmid, gdec = pl.pallas_call(
        functools.partial(results, scale),
        out_shape=(
            jax.ShapeDtypeStruct(features.shape, BF),
            jax.ShapeDtypeStruct(w_enc.shape, F32),
            jax.ShapeDtypeStruct(w_mid.shape, F32),
            jax.ShapeDtypeStruct(w_dec.shape, F32),
        ),
        in_specs=[anywhere] * 3,
        out_specs=[anywhere] + [vmem] * 3,
        scratch_shapes=[
            pltpu.VMEM(features.shape, BF),
            pltpu.VMEM((n1, 80, 128), BF),
            pltpu.VMEM((n2, 48, 128), BF),
            dma((4,)),
        ],
        compiler_params=pltpu.CompilerParams(vmem_limit_bytes=60 * 2**20),
    )(moved, a_sum, b_sum)
    return decoded, genc, gmid.transpose(0, 2, 1), gdec


def solution(mesh):
    placed = (P(None, "gz", "gy", None), P(), P(), P(), P(None, "gz", "gy", None))
    return jax.shard_map(
        local,
        mesh=mesh,
        in_specs=placed,
        out_specs=(P(None, "gz", "gy", None), P(), P(), P()),
        check_vma=False,
    )
```

```python
import functools

import jax
import jax.numpy as jnp
from jax import lax
from jax.experimental import pallas as pl
from jax.experimental.pallas import tpu as pltpu
from jax.sharding import PartitionSpec as P

MESH = pl.DeviceIdType.MESH
BF = jnp.bfloat16
F32 = jnp.float32
DIRECTIONS = [(a, b) for a in (-1, 0, 1) for b in (-1, 0, 1) if (a, b) != (0, 0)]


def iota(shape, dim):
    return lax.broadcasted_iota(jnp.int32, shape, dim)


def hot(mask):
    return jnp.where(mask, 1.0, 0.0).astype(BF)


def dot(a, b):
    return jnp.dot(a, b, preferred_element_type=F32)


def dot_nt(a, b):
    return lax.dot_general(a, b, (((1,), (1,)), ((), ())), preferred_element_type=F32)


def rows_to_cells(chans, height):
    n = chans * height
    r, s = iota((n, n), 0), iota((n, n), 1)
    return hot(s == (r % chans) * height + r // chans)


def cells_to_rows(chans, height):
    n = chans * height
    r, s = iota((n, n), 0), iota((n, n), 1)
    return hot(r == (s % chans) * height + s // chans)


def split_four(width):
    half = width // 2
    r, s = iota((width, 2 * width), 0), iota((width, 2 * width), 1)
    return hot(r == 2 * (s % half) - 1 + s // half)


def shift_parity(width):
    half = width // 2
    r, s = iota((width, width), 0), iota((width, width), 1)
    c = s % half
    first = (s < half) & (c > 0) & (r == half + c - 1)
    second = (s >= half) & (c < half - 1) & (r == c + 1)
    return hot(first | second)


def shift_both(half):
    r, s = iota((half, 2 * half), 0), iota((half, 2 * half), 1)
    return hot(((s < half) & (r == s - 1)) | ((s >= half) & (r == s - half + 1)))


def merge_parity(width):
    half = width // 2
    r, s = iota((width, width), 0), iota((width, width), 1)
    return hot(s == 2 * (r % half) + r // half)


def place(z, y):
    return (z - lax.rem(z, 2) + y // 2, 2 * lax.rem(y, 2) + lax.rem(z, 2))


def block(gz, gy):
    return gz - lax.rem(gz, 2) + lax.rem(gy, 2), 2 * lax.rem(gz, 2) + gy // 2


class Move:
    def __init__(self, src, dst, send, recv, peer, stays):
        self.src, self.dst, self.send, self.recv = src, dst, send, recv
        self.peer, self.stays = peer, stays

    def remote(self):
        return pltpu.make_async_remote_copy(
            src_ref=self.src, dst_ref=self.dst, send_sem=self.send, recv_sem=self.recv,
            device_id=self.peer, device_id_type=MESH,
        )

    def either(self, near, far):
        pl.when(self.stays)(lambda: near(pltpu.make_async_copy(self.src, self.dst, self.recv)))
        pl.when(jnp.logical_not(self.stays))(lambda: far(self.remote()))

    def start(self):
        self.either(lambda c: c.start(), lambda c: c.start())

    def wait_recv(self):
        self.either(lambda c: c.wait(), lambda c: c.wait_recv())

    def wait_send(self):
        pl.when(jnp.logical_not(self.stays))(lambda: self.remote().wait_send())


class Halo:
    def __init__(self, ref, send, recv, number, grid):
        self.ref, self.send, self.recv, self.number = ref, send, recv, number
        self.gz, self.gy, self.nz, self.ny = grid
        self.depth, self.height = ref.shape[0] - 2, ref.shape[1] - 2

    def exists(self, a, b):
        checks = []
        if a:
            checks.append(self.gz > 0 if a < 0 else self.gz < self.nz - 1)
        if b:
            checks.append(self.gy > 0 if b < 0 else self.gy < self.ny - 1)
        return functools.reduce(jnp.logical_and, checks)

    def source(self, d, n):
        return {-1: pl.ds(1, 1), 0: pl.ds(1, n), 1: pl.ds(n, 1)}[d]

    def target(self, d, n):
        return {-1: pl.ds(n + 1, 1), 0: pl.ds(1, n), 1: pl.ds(0, 1)}[d]

    def copy(self, i):
        a, b = DIRECTIONS[i]
        peer = place(lax.rem(self.gz + a + self.nz, self.nz), lax.rem(self.gy + b + self.ny, self.ny))
        return pltpu.make_async_remote_copy(
            src_ref=self.ref.at[self.source(a, self.depth), self.source(b, self.height)],
            dst_ref=self.ref.at[self.target(a, self.depth), self.target(b, self.height)],
            send_sem=self.send.at[self.number, i],
            recv_sem=self.recv.at[self.number, i],
            device_id=peer,
            device_id_type=MESH,
        )

    def start(self, listed=(1, 6, 3, 4, 0, 2, 5, 7)):
        for i in listed:
            pl.when(self.exists(*DIRECTIONS[i]))(lambda i=i: self.copy(i).start())

    def clear(self):
        for i, (a, b) in enumerate(DIRECTIONS):
            @pl.when(jnp.logical_not(self.exists(-a, -b)))
            def _(a=a, b=b):
                part = self.ref.at[self.target(a, self.depth), self.target(b, self.height)]
                part[...] = jnp.zeros(part.shape, part.dtype)

    def arrived(self):
        for i, (a, b) in enumerate(DIRECTIONS):
            pl.when(self.exists(-a, -b))(lambda i=i: self.copy(i).wait_recv())

    def sent(self):
        for i, (a, b) in enumerate(DIRECTIONS):
            pl.when(self.exists(a, b))(lambda i=i: self.copy(i).wait_send())


class Group:
    def __init__(self, size, me, peer, listed):
        self.size, self.me, self.peer, self.listed = size, me, peer, listed

    def others(self):
        return self.listed


class Total:
    def __init__(self, first, second, mine, one, two, whole, sems, final, fsem):
        self.final, self.fsem = final, fsem
        self.first, self.second = first, second
        self.mine, self.one, self.two, self.whole = mine, one, two, whole
        self.send1, self.recv1, self.send2, self.recv2, self.send3, self.recv3 = sems

    def copy(self, src, dst, send, recv, slot, peer):
        return pltpu.make_async_remote_copy(
            src_ref=src, dst_ref=dst, send_sem=send, recv_sem=recv,
            device_id=peer, device_id_type=MESH,
        )

    def step1(self, t, incoming):
        g = self.first
        slot = t if incoming else g.me
        return self.copy(self.mine.at[t], self.one.at[slot], self.send1.at[t], self.recv1.at[slot], slot, g.peer(t))

    def step2(self, t, incoming):
        g = self.second
        slot = t if incoming else g.me
        return self.copy(self.two.at[g.me], self.two.at[slot], self.send2.at[t], self.recv2.at[slot], slot, g.peer(t))

    def step3(self, t, incoming):
        g = self.first
        slot = t if incoming else g.me
        return self.copy(self.final, self.whole.at[slot], self.send3.at[t], self.recv3.at[slot], slot, g.peer(t))

    def start1(self):
        for t in self.first.others():
            self.step1(t, False).start()

    def start2(self):
        total = self.mine[self.first.me].astype(F32)
        for t in self.first.others():
            self.step1(t, True).wait_recv()
            total = total + self.one[t].astype(F32)
        self.two[self.second.me] = total.astype(BF)
        for t in self.second.others():
            self.step2(t, False).start()

    def start3(self):
        for t in self.second.others():
            self.step2(t, True).wait_recv()
        total = self.two[0].astype(F32)
        for t in range(1, self.second.size):
            total = total + self.two[t].astype(F32)
        self.final[...] = total.astype(BF)
        self.keep().start()
        for t in self.first.others():
            self.step3(t, False).start()

    def keep(self):
        return pltpu.make_async_copy(self.final, self.whole.at[self.first.me], self.fsem)

    def finish(self):
        self.keep().wait()
        for t in self.first.others():
            self.step3(t, True).wait_recv()

    def drain(self):
        for t in self.first.others():
            self.step1(t, False).wait_send()
            self.step3(t, False).wait_send()
        for t in self.second.others():
            self.step2(t, False).wait_send()


def pair(ref, z, y, step=1):
    a = ref[pl.ds(z, 3), pl.ds(y, 3)]
    b = ref[pl.ds(z, 3), pl.ds(y + step, 3)]
    rows = 9 * ref.shape[2]
    return jnp.concatenate([a.reshape(rows, ref.shape[3]), b.reshape(rows, ref.shape[3])], axis=1)


def silu_slope(value):
    sigma = 1.0 / (1.0 + jnp.exp(-value))
    return sigma * (1.0 + value * (1.0 - sigma))


def silu(value):
    return value / (1.0 + jnp.exp(-value))


def kernel(
    nz, ny,
    feat_ref, cot_ref, wenc_hbm, wmid_hbm, wdec_hbm,
    decoded_ref, a_whole, b_whole,
    fh, ch, sh, ph, oh, bh,
    fx, cx, sx, px, ox, bx,
    wenc_ref, wmid_ref, wdec_ref, wsem, we_ref, wm_ref, ws_ref, wc_ref, wb_ref, wp_ref, turned,
    slope, bskip, bsum, boxed, skips, benc, dec_acc, enc_acc, mid_acc, dplane,
    a_mine, a_one, a_two, b_mine, b_one, b_two, a_final, b_final, fsem,
    fin, cin, dout, msend, mrecv, hsend, hrecv, as1, ar1, as2, ar2, as3, ar3, bs1, br1, bs2, br2, bs3, br3,
):
    gz, gy = lax.axis_index("gz"), lax.axis_index("gy")
    vz, vy = block(gz, gy)
    stays = (vz == gz) & (vy == gy)
    c1, depth, height, width = feat_ref.shape
    half = width // 2
    c2 = bsum.shape[1]
    chigh = height // 2
    grid = (vz, vy, nz, ny)
    fhalo, chalo, shalo, phalo, ohalo, bhalo = [
        Halo(ref, hsend, hrecv, n, grid) for n, ref in enumerate((fh, ch, sh, ph, oh, bh))
    ]
    near, core = gz // 2, lax.rem(gy, 2)
    chip = ny // 2 * lax.rem(gz, 2) + gy // 2
    column = Group(
        2 * ny,
        2 * chip + core,
        lambda t: (gz - lax.rem(gz, 2) + t // ny, lax.rem(t, ny)),
        [
            2 * lax.rem(chip + d, ny) + lax.rem(core + e, 2)
            for d, e in ((2, 0), (2, 1), (1, 0), (3, 0), (1, 1), (3, 1), (0, 1))
        ],
    )
    side = 4
    far = {0: 0, 1: 1, 2: 2, 3: 1}
    steps = sorted(((a, b) for a in range(side) for b in range(side)), key=lambda s: -far[s[0]] - far[s[1]])
    plane = Group(
        nz // 2,
        near,
        lambda t: (2 * t + lax.rem(gz, 2), gy),
        [
            side * lax.rem(near // side + a, side) + lax.rem(lax.rem(near, side) + b, side)
            for a, b in steps[:-1]
        ],
    )

    barrier = pltpu.get_barrier_semaphore()
    away = vz + 2 * lax.rem(vz, 2) - 1
    arrivals = column.size + plane.size - 2
    for b in (-1, 0, 1):
        near = (away >= 0) & (away < nz) & (vy + b >= 0) & (vy + b < ny)
        arrivals = arrivals + jnp.where(near, 1, 0)

        @pl.when(near)
        def _(b=b):
            pl.semaphore_signal(barrier, inc=1, device_id=place(away, vy + b), device_id_type=MESH)
    for group in (column, plane):
        for t in group.others():
            pl.semaphore_signal(barrier, inc=1, device_id=group.peer(t), device_id_type=MESH)

    weights = [
        pltpu.make_async_copy(src, dst, wsem.at[n])
        for n, (src, dst) in enumerate(
            ((wenc_hbm, wenc_ref), (wmid_hbm, wmid_ref), (wdec_hbm, wdec_ref))
        )
    ]
    for copy in weights:
        copy.start()
    target = place(gz, gy)
    moves = [
        [
            Move(src.at[:, z], dst.at[:, z], msend.at[n, z], mrecv.at[n, z], target, stays)
            for z in range(depth)
        ]
        for n, (src, dst) in enumerate(((feat_ref, fin), (cot_ref, cin)))
    ]
    to_cells = rows_to_cells(c1, height)

    def take(n, src, dst, halo):
        for z in range(depth):
            moves[n][z].wait_recv()
            own = src[:, z].astype(F32).reshape(c1 * height, width).astype(BF)
            own = dot(to_cells, own).astype(BF).reshape(height, c1, width)
            dst[1 + z, pl.ds(1, height)] = own
            halo.start((1, 0, 2) if z == 0 else (6, 5, 7, 3, 4))

    pl.semaphore_wait(barrier, arrivals)
    for listed in moves:
        for copy in listed:
            copy.start()
    for halo in (fhalo, chalo, shalo, phalo, ohalo, bhalo):
        halo.clear()
    a_mine[...] = jnp.zeros(a_mine.shape, BF)
    b_mine[...] = jnp.zeros(b_mine.shape, BF)
    boxed[...] = jnp.zeros(boxed.shape, BF)
    ox[...] = jnp.zeros(ox.shape, BF)
    bx[...] = jnp.zeros(bx.shape, BF)
    for copy in weights:
        copy.wait()
    prepare(wenc_ref, wmid_ref, wdec_ref, we_ref, wm_ref, ws_ref, wc_ref, wb_ref, wp_ref, turned)
    px[...] = jnp.zeros(px.shape, BF)
    dec_acc[...] = jnp.zeros(dec_acc.shape, F32)
    enc_acc[...] = jnp.zeros(enc_acc.shape, F32)
    mid_acc[...] = jnp.zeros(mid_acc.shape, F32)
    take(0, fin, fh, fhalo)
    take(1, cin, ch, chalo)

    def four(src, dst):
        spread = split_four(width)

        def body(z, carry):
            rows = src[z].reshape((height + 2) * c1, width)
            out = dot(rows, spread).astype(BF).reshape(height + 2, c1, 2 * width)
            for j in range(4):
                dst[z, :, j * c1 : (j + 1) * c1, :] = out[:, :, j * half : (j + 1) * half]
            return carry

        lax.fori_loop(0, depth + 2, body, 0)

    fhalo.arrived()
    four(fh, fx)

    def encode(yc, carry):
        pool = jnp.zeros((c1, half), F32)
        for z in range(depth):
            pre = dot(we_ref[...], pair(fx, z, 2 * yc))
            act = silu(pre).astype(BF)
            der = silu_slope(pre)
            for p in range(2):
                cell = act[:, p * half : (p + 1) * half]
                slope[z, 2 * yc + p] = der[:, p * half : (p + 1) * half]
                for q in range(2):
                    part = cell[q * c1 : (q + 1) * c1]
                    sh[1 + z, 1 + 2 * yc + p, :, q * half : (q + 1) * half] = part
                    skips[z, 2 * yc + p, q * c1 : (q + 1) * c1, :] = part
                    pool = pool + part.astype(F32)
        ph[1, 1 + yc] = (pool * 0.125).astype(BF)
        return carry

    lax.fori_loop(0, chigh, encode, 0)
    phalo.start()

    chalo.arrived()
    four(ch, cx)

    def backward(yc, carry):
        low = jnp.zeros((c2, half), F32)
        for z in range(depth):
            out = dot(wb_ref[...], pair(cx, z, 2 * yc))
            for p in range(2):
                for q in range(2):
                    part = out[q * (c1 + c2) : (q + 1) * (c1 + c2), p * half : (p + 1) * half]
                    low = low + part[:c2]
                    bskip[z, 2 * yc + p, q * c1 : (q + 1) * c1, :] = part[c2:]
        bsum[yc] = low
        return carry

    lax.fori_loop(0, chigh, backward, 0)

    def box(yc, carry):
        for w in range(3):
            low = cx[w, pl.ds(2 * yc, 4)].astype(F32) + cx[w + 1, pl.ds(2 * yc, 4)].astype(F32)
            for v in range(3):
                both = low[v] + low[v + 1]
                boxed[pl.ds((3 * w + v) * 3 * c1, 3 * c1), pl.ds(pl.multiple_of(yc * half, half), half)] = (
                    both[: 3 * c1] + both[c1:]
                ).astype(BF)
        return carry

    lax.fori_loop(0, chigh, box, 0)

    def store(dst, n, piece):
        each = dst.shape[1] // 16
        dst[n // each, (n % each) * 16 : (n % each + 1) * 16, :] = piece

    def decoder_grad(yc, carry):
        for z in range(depth):
            own = jnp.concatenate([skips[z, 2 * yc], skips[z, 2 * yc + 1]], axis=1)
            dec_acc[...] += dot_nt(own, pair(cx, z, 2 * yc))
        return carry

    lax.fori_loop(0, chigh, decoder_grad, 0)

    def pack(acc, dst, first):
        for kk in range(9):
            even = acc[0:c1, kk * 128 : (kk + 1) * 128]
            odd = acc[c1 : 2 * c1, kk * 128 : (kk + 1) * 128]
            piece = (even + pltpu.roll(odd, 128 - c1, 1)).astype(BF)
            for h in range(2):
                store(dst, first + 2 * kk + h, piece[h * 16 : (h + 1) * 16])

    pack(dec_acc, a_mine, 56)

    sides = shift_both(half)

    def three(src, dst):
        chans = src.shape[2]
        rows = src[...].reshape(src.shape[0] * src.shape[1] * chans, half)
        out = dot(rows, sides).astype(BF).reshape(src.shape[0], src.shape[1], chans, 2 * half)
        dst[:, :, 0:chans, :] = out[..., :half]
        dst[:, :, chans : 2 * chans, :] = src[...]
        dst[:, :, 2 * chans : 3 * chans, :] = out[..., half:]

    phalo.arrived()
    three(ph, px)
    for yc in range(0, chigh, 2):
        pre = dot(wm_ref[...], pair(px, 0, yc))
        for p in range(2):
            cell = pre[:, p * half : (p + 1) * half]
            act = silu(cell).astype(BF)
            oh[1, 1 + yc + p] = act
            bh[1, 1 + yc + p] = (silu_slope(cell) * bsum[yc + p]).astype(BF)
    bhalo.start()
    ohalo.start()
    shalo.start()

    own = jnp.concatenate([oh[1, 1 + yc] for yc in range(chigh)], axis=1)
    none = jnp.zeros_like(own)
    low = dot_nt(boxed[: 14 * c1], jnp.concatenate([own, none], axis=0)) + dot_nt(
        boxed[14 * c1 :], jnp.concatenate([none, own], axis=0)
    )
    low = low.astype(BF)
    for n in range(28):
        store(a_mine, n, low[n * 16 : (n + 1) * 16])

    for yc in range(0, chigh, 2):
        own = jnp.concatenate([bh[1, 1 + yc], bh[1, 2 + yc]], axis=1)
        mid_acc[...] += dot_nt(pair(px, 0, yc), jnp.concatenate([own, own], axis=0))

    def mid_rows(k):
        row = (k // 3) * 128 + (k % 3) * c1
        return mid_acc[row : row + c1, :]

    first = iota((c1, 128), 1) < c2
    for d in range(14):
        piece = jnp.where(first, mid_rows(d), mid_rows(d + 14)) if d < 13 else mid_rows(d)
        piece = piece.astype(BF)
        for h in range(2):
            store(a_mine, 28 + 2 * d + h, piece[h * 16 : (h + 1) * 16])
    a_total = Total(plane, column, a_mine, a_one, a_two, a_whole, (as1, ar1, as2, ar2, as3, ar3), a_final, fsem.at[0])
    a_total.start1()

    bhalo.arrived()
    three(bh, bx)
    for yc in range(0, chigh, 2):
        pool = dot(wp_ref[...], pair(bx, 0, yc)) * 0.125
        for p in range(2):
            up = pool[:, p * half : (p + 1) * half]
            up = jnp.concatenate([up, up], axis=0)
            for z in range(depth):
                for r in range(2):
                    y = 2 * (yc + p) + r
                    benc[z, y] = (slope[z, y] * (bskip[z, y] + up)).astype(BF)

    def encoder_grad(yc, carry):
        for z in range(depth):
            own = jnp.concatenate([benc[z, 2 * yc], benc[z, 2 * yc + 1]], axis=1)
            enc_acc[...] += dot_nt(own, pair(fx, z, 2 * yc))
        return carry

    lax.fori_loop(0, chigh, encoder_grad, 0)
    pack(enc_acc, b_mine, 0)
    b_total = Total(column, plane, b_mine, b_one, b_two, b_whole, (bs1, br1, bs2, br2, bs3, br3), b_final, fsem.at[1])
    b_total.start1()
    a_total.start2()

    shalo.arrived()
    turn = shift_parity(width)

    def four_skip(z, carry):
        rows = sh[z].reshape((height + 2) * c1, width)
        out = dot(rows, turn).astype(BF).reshape(height + 2, c1, width)
        sx[z, :, 0:c1, :] = out[:, :, :half]
        sx[z, :, c1 : 2 * c1, :] = sh[z, :, :, 0:half]
        sx[z, :, 2 * c1 : 3 * c1, :] = sh[z, :, :, half:width]
        sx[z, :, 3 * c1 : 4 * c1, :] = out[:, :, half:]
        return carry

    lax.fori_loop(0, depth + 2, four_skip, 0)
    ohalo.arrived()
    three(oh, ox)
    b_total.start2()
    a_total.start3()

    def decode(yc, carry):
        for z in range(depth):
            out = dot(ws_ref[...], pair(sx, z, 2 * yc))
            for p in range(2):
                field = ox[pl.ds(z, 2), pl.ds(yc + p, 2)].reshape(4 * 4 * c2, half)
                row = (out[:, p * half : (p + 1) * half] + dot(wc_ref[2 * z + p], field)).astype(BF)
                for q in range(2):
                    dplane[z, 2 * yc + p, :, q * half : (q + 1) * half] = row[q * c1 : (q + 1) * c1]
        return carry

    lax.fori_loop(0, chigh, decode, 0)
    to_rows = cells_to_rows(c1, height)
    merge = merge_parity(width)
    back = [
        Move(dout.at[:, z], decoded_ref.at[:, z], msend.at[2, z], mrecv.at[2, z], (vz, vy), stays)
        for z in range(depth)
    ]
    for z in range(depth):
        rows = dplane[z].reshape(height * c1, width)
        rows = dot(rows, merge).astype(BF)
        dout[:, z] = dot(to_rows, rows).reshape(c1, height, width).astype(BF)
        back[z].start()

    b_total.start3()
    a_total.finish()
    b_total.finish()
    for copy in back:
        copy.wait_recv()
    for copy in moves[0] + moves[1] + back:
        copy.wait_send()
    for halo in (fhalo, chalo, shalo, phalo, ohalo, bhalo):
        halo.sent()
    a_total.drain()
    b_total.drain()


def results(
    scale, moved_hbm, a_hbm, b_hbm, decoded_ref, genc_ref, gmid_ref, gdec_ref, moved_ref, a_ref, b_ref, sem
):
    copies = [
        pltpu.make_async_copy(src, dst, sem.at[n])
        for n, (src, dst) in enumerate(((a_hbm, a_ref), (b_hbm, b_ref), (moved_hbm, moved_ref)))
    ]
    for copy in copies:
        copy.start()
    c1, c2 = genc_ref.shape[1], gmid_ref.shape[2]

    def load(src, n):
        each = src.shape[1] // 16
        return src[n // each, (n % each) * 16 : (n % each + 1) * 16, :].astype(F32) * scale

    def both(src, n):
        return jnp.concatenate([load(src, n), load(src, n + 1)], axis=0)

    copies[2].wait()
    out = pltpu.make_async_copy(moved_ref, decoded_ref, sem.at[3])
    out.start()
    copies[0].wait()
    copies[1].wait()
    for d in range(14):
        low, mid = both(a_ref, 2 * d), both(a_ref, 28 + 2 * d)
        for h in range(2 if d < 13 else 1):
            gdec_ref[26 - d - 14 * h, :, 0:c2] = low[:, h * c2 : (h + 1) * c2]
            gmid_ref[d + 14 * h] = mid[:, h * c2 : (h + 1) * c2]
    for kk in range(9):
        skip, enc = both(a_ref, 56 + 2 * kk).T, both(b_ref, 2 * kk)
        for kx in range(3):
            gdec_ref[3 * (8 - kk) + 2 - kx, :, c2 : c2 + c1] = skip[kx * c1 : (kx + 1) * c1]
            genc_ref[3 * kk + kx] = enc[:, kx * c1 : (kx + 1) * c1]
    out.wait()


def split_weights(w_ref, kx):
    return jnp.concatenate([w_ref[3 * kk + kx] for kk in range(9)], axis=0)


def fine_weights(w_ref, first, dst):
    outs, ins, n = w_ref.shape[1], w_ref.shape[2], dst.shape[1] // 36
    total = jnp.zeros((9 * outs, 8 * n), F32)
    for kx in range(3):
        r, c = iota((ins, 8 * n), 0), iota((ins, 8 * n), 1)
        px, jx, i = c // (4 * n), (c // n) % 4, c % n
        total = total + dot(split_weights(w_ref, kx), hot((jx == kx + px) & (r == first + i)))
    total = total.astype(BF)
    for kk in range(9):
        for p in range(2):
            dst[p * outs : (p + 1) * outs, kk * 4 * n : (kk + 1) * 4 * n] = total[
                kk * outs : (kk + 1) * outs, p * 4 * n : (p + 1) * 4 * n
            ]


def prepare(wenc_ref, wmid_ref, wdec_ref, we_ref, wm_ref, ws_ref, wc_ref, wb_ref, wp_ref, turned):
    c1, c2 = wmid_ref.shape[1:]
    fine_weights(wenc_ref, 0, we_ref)
    fine_weights(wdec_ref, c2, ws_ref)

    blank = jnp.zeros((c1, c2), BF)
    rows = [wmid_ref[3 * kk + kx] if kx < 3 else blank for kk in range(9) for kx in range(4)]
    pick = hot(iota((c2, c2), 0) == iota((c2, c2), 1))
    wm_ref[...] = dot_nt(pick, jnp.concatenate(rows, axis=0)).astype(BF)
    total = jnp.zeros((9 * c1, 4 * c2), F32)
    for kx in range(3):
        rows = jnp.concatenate([wmid_ref[26 - 3 * kk - kx] for kk in range(9)], axis=0)
        r, c = iota((c2, 4 * c2), 0), iota((c2, 4 * c2), 1)
        total = total + dot(rows, hot(c == kx * c2 + r))
    total = total.astype(BF)
    for kk in range(9):
        wp_ref[:, kk * 4 * c2 : (kk + 1) * 4 * c2] = total[kk * c1 : (kk + 1) * c1]

    total = jnp.zeros((9 * c1, 8 * c2), F32)
    for kx in range(3):
        r, c = iota((c1 + c2, 8 * c2), 0), iota((c1 + c2, 8 * c2), 1)
        px, slot, i = c // (4 * c2), (c // c2) % 4, c % c2
        wanted = (kx + px + 1) // 2
        total = total + dot(split_weights(wdec_ref, kx), hot((slot == wanted) & (r == i)))
    parts = [[[0], [1, 2]], [[0, 1], [2]]]
    for pz in range(2):
        for py in range(2):
            for cz in range(2):
                for cy in range(2):
                    part = sum(
                        total[(3 * kz + ky) * c1 : (3 * kz + ky + 1) * c1]
                        for kz in parts[pz][cz]
                        for ky in parts[py][cy]
                    ).astype(BF)
                    at = (2 * cz + cy) * 4 * c2
                    for p in range(2):
                        wc_ref[2 * pz + py, p * c1 : (p + 1) * c1, at : at + 4 * c2] = part[
                            :, p * 4 * c2 : (p + 1) * 4 * c2
                        ]

    turned[...] = jnp.zeros(turned.shape, BF)
    blank = jnp.zeros((c1, c1 + c2), BF)
    for kk in range(9):
        for p in range(2):
            for jx in range(4):
                kx = jx - p
                value = wdec_ref[26 - 3 * kk - kx] if 0 <= kx < 3 else blank
                row = kk * 4 * c1 + jx * c1
                turned[row : row + c1, p * 128 : p * 128 + c1 + c2] = value
    r, c = iota((2 * (c1 + c2), 256), 0), iota((2 * (c1 + c2), 256), 1)
    pick = hot(c == (r // (c1 + c2)) * 128 + r % (c1 + c2))
    wb_ref[...] = dot_nt(pick, turned[...]).astype(BF)


def local(features, w_enc, w_mid, w_dec, cotangent):
    nz, ny = lax.axis_size("gz"), lax.axis_size("gy")
    c1, depth, height, width = features.shape
    c2 = w_mid.shape[1]
    w_mid = w_mid.transpose(0, 2, 1)
    half, ch = width // 2, height // 2
    assert nz == 32 and ny == 4 and depth == 2 and c1 == 32 and c2 == 64 and half == 128
    scale = (depth * nz * height * ny * width) ** (-0.5)
    n1, n2 = nz // 2, 2 * ny
    vmem = pl.BlockSpec(memory_space=pltpu.VMEM)
    anywhere = pl.BlockSpec(memory_space=pl.ANY)
    dma = pltpu.SemaphoreType.DMA
    fine, coarse = (depth + 2, height + 2), (3, ch + 2)
    moved, a_sum, b_sum = pl.pallas_call(
        functools.partial(kernel, nz, ny),
        out_shape=(
            jax.ShapeDtypeStruct(features.shape, BF),
            jax.ShapeDtypeStruct((n1, 80, 128), BF),
            jax.ShapeDtypeStruct((n2, 48, 128), BF),
        ),
        in_specs=[anywhere] * 5,
        out_specs=[anywhere] * 3,
        scratch_shapes=[
            pltpu.VMEM(fine + (c1, width), BF),
            pltpu.VMEM(fine + (c1, width), BF),
            pltpu.VMEM(fine + (c1, width), BF),
            pltpu.VMEM(coarse + (c1, half), BF),
            pltpu.VMEM(coarse + (c2, half), BF),
            pltpu.VMEM(coarse + (c2, half), BF),
            pltpu.VMEM(fine + (4 * c1, half), BF),
            pltpu.VMEM(fine + (4 * c1, half), BF),
            pltpu.VMEM(fine + (4 * c1, half), BF),
            pltpu.VMEM(coarse + (4 * c1, half), BF),
            pltpu.VMEM(coarse + (4 * c2, half), BF),
            pltpu.VMEM(coarse + (4 * c2, half), BF),
            pltpu.VMEM(w_enc.shape, BF),
            pltpu.VMEM(w_mid.shape, BF),
            pltpu.VMEM(w_dec.shape, BF),
            dma((3,)),
            pltpu.VMEM((2 * c1, 36 * c1), BF),
            pltpu.VMEM((c2, 36 * c1), BF),
            pltpu.VMEM((2 * c1, 36 * c1), BF),
            pltpu.VMEM((4, 2 * c1, 16 * c2), BF),
            pltpu.VMEM((2 * (c1 + c2), 36 * c1), BF),
            pltpu.VMEM((c1, 36 * c2), BF),
            pltpu.VMEM((36 * c1, 256), BF),
            pltpu.VMEM((depth, height, 2 * c1, half), F32),
            pltpu.VMEM((depth, height, 2 * c1, half), F32),
            pltpu.VMEM((ch, c2, half), F32),
            pltpu.VMEM((28 * c1, ch * half), BF),
            pltpu.VMEM((depth, height, 2 * c1, half), BF),
            pltpu.VMEM((depth, height, 2 * c1, half), BF),
            pltpu.VMEM((2 * c1, 9 * 128), F32),
            pltpu.VMEM((2 * c1, 9 * 128), F32),
            pltpu.VMEM((9 * 128, 128), F32),
            pltpu.VMEM((depth, height, c1, width), BF),
            pltpu.VMEM((n1, 80, 128), BF),
            pltpu.VMEM((n1, 80, 128), BF),
            pltpu.VMEM((n2, 80, 128), BF),
            pltpu.VMEM((n2, 48, 128), BF),
            pltpu.VMEM((n2, 48, 128), BF),
            pltpu.VMEM((n1, 48, 128), BF),
            pltpu.VMEM((80, 128), BF),
            pltpu.VMEM((48, 128), BF),
            dma((2,)),
            pltpu.VMEM(features.shape, BF),
            pltpu.VMEM(features.shape, BF),
            pltpu.VMEM(features.shape, BF),
            dma((3, 2)), dma((3, 2)), dma((6, 8)), dma((6, 8)),
            dma((n1,)), dma((n1,)), dma((n2,)), dma((n2,)), dma((n1,)), dma((n1,)),
            dma((n2,)), dma((n2,)), dma((n1,)), dma((n1,)), dma((n2,)), dma((n2,)),
        ],
        compiler_params=pltpu.CompilerParams(
            collective_id=0, has_side_effects=True, vmem_limit_bytes=60 * 2**20
        ),
    )(features, cotangent, w_enc, w_mid, w_dec)
    decoded, genc, gmid, gdec = pl.pallas_call(
        functools.partial(results, scale),
        out_shape=(
            jax.ShapeDtypeStruct(features.shape, BF),
            jax.ShapeDtypeStruct(w_enc.shape, F32),
            jax.ShapeDtypeStruct(w_mid.shape, F32),
            jax.ShapeDtypeStruct(w_dec.shape, F32),
        ),
        in_specs=[anywhere] * 3,
        out_specs=[anywhere] + [vmem] * 3,
        scratch_shapes=[
            pltpu.VMEM(features.shape, BF),
            pltpu.VMEM((n1, 80, 128), BF),
            pltpu.VMEM((n2, 48, 128), BF),
            dma((4,)),
        ],
        compiler_params=pltpu.CompilerParams(vmem_limit_bytes=60 * 2**20),
    )(moved, a_sum, b_sum)
    return decoded, genc, gmid.transpose(0, 2, 1), gdec


def solution(mesh):
    placed = (P(None, "gz", "gy", None), P(), P(), P(), P(None, "gz", "gy", None))
    return jax.shard_map(
        local,
        mesh=mesh,
        in_specs=placed,
        out_specs=(P(None, "gz", "gy", None), P(), P(), P()),
        check_vma=False,
    )
```
